128 devices in a mesh: sect: 16 (over y, x), lane: 8 (over z, core).
Axes of the slice: x: 4, y: 4, z: 4, core: 2. Of those that a mesh axis runs over, the one named last changes fastest.
Arguments:
- atm_state: bfloat16 [524288, 512], P(('sect', 'lane')), may hold values from -6 to 6
- profile: float32 [128], replicated, may hold values from 0.02 to 0.5
- mixing: bfloat16 [4, 128, 128], replicated, may hold values from -0.5 to 0.5
- radiation: float32 [4, 524288], P(None, ('sect', 'lane')), may hold values from 0 to 1
- ocean_mask: int32 [524288], P(('sect', 'lane')), may hold values 0 or 1
- tile_src: int32 [32768, 4], P(('sect', 'lane')), may hold values from 0 to 127, all different within a row; in each aligned block of 256 rows (0 to 255, 256 to 511, ...) at most 16 rows name the same one
- tile_elem: int32 [32768, 4], P(('sect', 'lane')), may hold values from 0 to 255
- remap_w: float32 [32768, 64, 128], P(('sect', 'lane')), may hold values from 0.05 to 1
- slope_class: int32 [32768, 128], P(('sect', 'lane')), may hold values from 0 to 7
- aspect_class: int32 [32768, 128], P(('sect', 'lane')), may hold values from 0 to 7
- sky_view: float32 [32768, 128], P(('sect', 'lane')), may hold values from 0.6 to 1
- albedo: float32 [32768, 128], P(('sect', 'lane')), may hold values from 0.1 to 0.4
- sun_cos: float32 [32768], P(('sect', 'lane')), may hold values from 0.25 to 1
- sun_azimuth: float32 [32768], P(('sect', 'lane')), may hold values from -3.140625 to 3.140625
Outputs:
- atm_out: bfloat16 [524288, 512], P(('sect', 'lane'))
- land_temp: float32 [32768, 128], P(('sect', 'lane'))
- col_flux: float32 [8, 524288], P(None, ('sect', 'lane'))
The draws below stay inside these ranges and needn't reach their ends.
Inputs may be any that keep to these rules, and one draw needn't show every extreme that they name: `tile_src`: each tile names 4 different atmosphere devices; among the tiles of one device no atmosphere device is named more than 16 times, a bound that some block reaches.
All inputs are finite; a program needn't handle non-finite values. No bound on the sum of `ocean_mask` on one device may be relied on, other than what follows from the above.
Results may differ from the reference program's by a relative error of at most 0.001.
The reference program's roundings to bfloat16 on the way (of `mixed`) count: a program that leaves them out, or rounds other values in their place, can miss the bound.
Values sent between devices are 32-bit elements; how exact they have to be, the bound alone decides.
No kernel may reach another device: no remote copies, remote signals or barrier semaphores. Data moves between devices by JAX's collectives and lax.ppermute only.
A program may use at most 128 MiB of HBM per device.

```python
import math
import jax
import jax.numpy as jnp
import numpy as np
from jax import lax

ELEM_DEV = 256
GLL = 16
LEV = 128
NV = 4
NF = 8
NFLUX = 8
SUB = 4
NEWTON = 2
TILE_DEV = 256
UNIT = 128
REF = 4
NSLOPE = 8
NASPECT = 8
CAP = 16
TILES = 32768
ACOLS = 524288
N_SECT = 16
N_LANE = 8
DEVICES = 128


def with_ends(entries, key, smallest, largest):
    shape = entries.shape
    spot = [jax.random.randint(jax.random.fold_in(key, axis), (), 0, shape[axis]) for axis in range(len(shape))]
    entries = entries.at[tuple(spot)].set(smallest)
    longest = shape.index(max(shape))
    spot[longest] = (spot[longest] + 1) % shape[longest]
    return entries.at[tuple(spot)].set(largest)


def levels(own_key, shape, split, least, high):
    factor_of, own = 1.0, jax.random.fold_in(own_key, 6)
    for position, blocks in split:
        heights = jnp.exp(jax.random.uniform(jax.random.fold_in(own, position), (blocks,), jnp.float32, least / len(split), high / len(split)))
        factor_of = factor_of * jnp.repeat(heights, shape[position] // blocks).reshape([-1 if axis == position else 1 for axis in range(len(shape))])
    return factor_of


def routed_block(stream_key, own, number, rows, number_of, top, reach, slope):
    order = jax.random.permutation(stream_key, number_of)
    packed, ordinary = load_shares(number_of, rows * top, reach, slope, True), load_shares(number_of, rows * top, reach, slope, False)
    places = jnp.arange(number_of)

    def named(sizes, rotation):
        used = int((sizes > 0).sum())
        fixed = max(1, used // 4)
        passed = fixed + (places - fixed + rotation * (used - fixed)) % max(1, number_of - fixed)
        return jnp.zeros((number_of,), jnp.int32).at[order[jnp.where(places < fixed, places, passed)]].set(jnp.asarray(sizes, jnp.int32))

    sizes = jnp.where(number % 4 == 0, named(packed, number // 4), named(ordinary, number - number // 4 - 1))
    mixed = jax.random.permutation(jax.random.fold_in(own, 3), number_of)
    donor, receiver = mixed[0:number_of // 2 * 2:2], mixed[1:number_of // 2 * 2:2]
    slack = jnp.minimum(sizes[donor] - 1, reach - sizes[receiver]) // 2
    slack = jnp.where((donor == order[0]) | (receiver == order[0]) | (sizes[receiver] == 0), 0, jnp.maximum(slack, 0))
    passed = jax.random.randint(jax.random.fold_in(own, 4), (number_of // 2,), 0, 1 << 20) % (slack + 1)
    sizes = sizes.at[donor].add(-passed).at[receiver].add(passed)
    members = jnp.searchsorted(jnp.cumsum(sizes), jnp.arange(rows * top), side="right").astype(jnp.int32)
    table = members.reshape(top, rows).T
    table = table[jax.random.permutation(jax.random.fold_in(own, 1), rows)]
    rotation = jax.random.randint(jax.random.fold_in(own, 2), (rows, 1), 0, top)
    return jnp.take_along_axis(table, (jnp.arange(top)[None, :] + rotation) % top, axis=1)


def load_shares(number_of, total, most, skew, full):
    loads = [(1 << 20) // math.isqrt(rank ** skew) + 1 for rank in range(1, number_of + 1)]
    largest = most if full else min(most, max(-(-total // number_of), total * loads[0] // sum(loads)))
    least = 1 if total - largest >= number_of - 1 else 0
    given, spare = [largest] + [least] * (number_of - 1), total - largest - least * (number_of - 1)
    while spare > 0:
        movable = [i for i in range(1, number_of) if given[i] < largest] or [i for i in range(1, number_of) if given[i] < most]
        pool, left = sum([loads[i] for i in movable]), spare
        for i in movable:
            extra = min(most - given[i], max(1, left * loads[i] // pool), spare)
            given[i] = given[i] + extra
            spare = spare - extra
    return np.array(given)


def bell_draw(key, shape, deviation, reach, shards=(), kind=jnp.bfloat16):
    array = jax.random.normal(key, shape, jnp.float32) * deviation
    if len(shards) > 0:
        array = levels(key, shape, shards, -0.22, 0.18) * array
    return jnp.clip(array, min=-reach, max=reach).astype(kind)


def setup_inputs(seed: int = 0) -> dict:
    keys = jax.random.split(jax.random.key(seed), 15)
    atm_state = bell_draw(keys[0], (ACOLS, NV * LEV), 1.0, 6.0, ((0, 128),))
    profile = jnp.clip(jnp.exp(jax.random.uniform(keys[1], (LEV,), jnp.float32, math.log(0.02), math.log(0.5))), 0.02, 0.5)
    mixing = bell_draw(keys[2], (NV, LEV, LEV), LEV ** -0.5, 0.5)
    radiation = jnp.clip(1.0 * jax.random.uniform(keys[3], (4, ACOLS), jnp.float32) ** levels(keys[3], (4, ACOLS), ((1, 128),), -0.2, 0.2), 0.0, 1.0)
    ocean_mask = with_ends((jax.random.randint(keys[4], (ACOLS,), 0, 2) < 1).astype(jnp.int32), jax.random.fold_in(keys[4], 1), 0, 1)
    tile_src_keys = jax.random.split(jax.random.fold_in(keys[5], 1), TILES // TILE_DEV)
    tile_src_turns = jax.random.permutation(jax.random.fold_in(keys[5], 3), TILES // TILE_DEV)
    tile_src = jax.vmap(lambda own, number: routed_block(jax.random.fold_in(keys[5], 2), own, number, TILE_DEV, DEVICES, REF, CAP, 2))(tile_src_keys, tile_src_turns).reshape((TILES, REF))
    tile_elem = with_ends(jax.random.randint(keys[6], (TILES, REF), 0, ELEM_DEV), jax.random.fold_in(keys[6], 1), 0, ELEM_DEV - 1).astype(jnp.int32)
    remap_w = jnp.clip(jnp.exp(math.log(1.0) - 2.9957323 * jax.random.uniform(keys[7], (TILES, REF * GLL, UNIT), jnp.float32) ** levels(keys[7], (TILES, REF * GLL, UNIT), ((0, 128),), -0.2, 0.2)), 0.05, 1.0)
    slope_class = with_ends(jax.random.randint(keys[8], (TILES, UNIT), 0, NSLOPE), jax.random.fold_in(keys[8], 1), 0, NSLOPE - 1).astype(jnp.int32)
    aspect_class = with_ends(jax.random.randint(keys[9], (TILES, UNIT), 0, NASPECT), jax.random.fold_in(keys[9], 1), 0, NASPECT - 1).astype(jnp.int32)
    sky_view = jnp.clip(0.6 + 0.39999998 * jax.random.uniform(keys[10], (TILES, UNIT), jnp.float32) ** levels(keys[10], (TILES, UNIT), ((0, 128),), -0.2, 0.2), 0.6, 1.0)
    albedo = jnp.clip(0.1 + 0.3 * jax.random.uniform(keys[11], (TILES, UNIT), jnp.float32) ** levels(keys[11], (TILES, UNIT), ((0, 128),), -0.2, 0.2), 0.1, 0.4)
    sun_cos = jnp.clip(0.25 + 0.75 * jax.random.uniform(keys[12], (TILES,), jnp.float32) ** levels(keys[12], (TILES,), ((0, 128),), -0.2, 0.2), 0.25, 1.0)
    sun_azimuth = jnp.clip(jax.random.uniform(keys[13], (TILES,), jnp.float32, -3.140625, 3.140625), -3.140625, 3.140625)
    return {"atm_state": atm_state, "profile": profile, "mixing": mixing, "radiation": radiation, "ocean_mask": ocean_mask, "tile_src": tile_src, "tile_elem": tile_elem, "remap_w": remap_w, "slope_class": slope_class, "aspect_class": aspect_class, "sky_view": sky_view, "albedo": albedo, "sun_cos": sun_cos, "sun_azimuth": sun_azimuth}


def drivers(fields):
    air_temp = 1.0 + 0.05 * jnp.tanh(fields[0])
    air_humid = 0.02 * jax.nn.sigmoid(fields[1])
    wind_speed = jnp.sqrt(1.0 + fields[2] * fields[2] + fields[3] * fields[3])
    return (air_temp, air_humid, wind_speed, 1.5 * fields[4], 0.5 * fields[5], 0.6 + 0.3 * fields[6], fields[7])

def surface_fluxes(surface, fields, absorbed, reflected, wetness, stack_axis):
    air_temp, air_humid, wind_speed = drivers(fields)[:3]
    heat_coef = 0.1 * wind_speed
    vapor_coef = 0.25 * wind_speed * wetness
    saturation = 0.02 * jnp.exp(17.0 * (surface - 1.0))
    sensible = heat_coef * (surface - air_temp)
    latent = vapor_coef * (saturation - air_humid)
    upward = 0.95 * surface ** 4
    drag = 0.05 * wind_speed
    return jnp.stack([sensible, latent, upward, reflected, drag * fields[2], drag * fields[3], 0.4 * latent, absorbed - upward - sensible - latent], axis=stack_axis)

def land_balance(raw, sky_view, albedo, slope_class, aspect_class, sun_cos, sun_azimuth):
    fields = [raw[:, field_index] for field_index in range(NF)]
    air_temp, air_humid, wind_speed, direct_sw, diffuse_sw, longwave, wetness = drivers(fields)
    cosine = sun_cos[:, None]
    sine = jnp.sqrt(1.0 - cosine * cosine)
    slope_angle = slope_class.astype(jnp.float32) * 0.1
    aspect_angle = aspect_class.astype(jnp.float32) * (2.0 * math.pi / NASPECT)
    incidence = jnp.maximum(0.0, jnp.cos(slope_angle) * cosine + jnp.sin(slope_angle) * sine * jnp.cos(sun_azimuth[:, None] - aspect_angle))
    shortwave = direct_sw * incidence / cosine + diffuse_sw * sky_view
    absorbed = (1.0 - albedo) * shortwave + 0.95 * longwave * sky_view
    heat_coef = 0.1 * wind_speed
    vapor_coef = 0.25 * wind_speed * wetness
    surface = air_temp
    for iteration in range(NEWTON):
        saturation = 0.02 * jnp.exp(17.0 * (surface - 1.0))
        imbalance = absorbed - 0.95 * surface ** 4 - heat_coef * (surface - air_temp) - vapor_coef * (saturation - air_humid)
        derivative = -3.8 * surface ** 3 - heat_coef - 17.0 * vapor_coef * saturation
        surface = surface - imbalance / derivative
    return (surface, surface_fluxes(surface, fields, absorbed, albedo * shortwave, wetness, 1))

def ocean_fluxes(forcing):
    fields = [forcing[field_index] for field_index in range(NF)]
    direct_sw, diffuse_sw, longwave = drivers(fields)[3:6]
    shortwave = direct_sw + diffuse_sw
    absorbed = 0.94 * shortwave + 0.95 * longwave
    return surface_fluxes(jnp.ones_like(fields[0]), fields, absorbed, 0.06 * shortwave, jnp.ones_like(fields[0]), 0)

def forcing_fields(atm_state, profile, radiation):
    columns = atm_state.shape[0]
    state = atm_state.astype(jnp.float32).reshape(columns, NV, LEV)
    means = lax.optimization_barrier(jnp.sum(state * profile, axis=2))
    return jnp.concatenate([means.T, radiation], axis=0)

def remap_in(requested, remap_w):
    normal = remap_w / lax.optimization_barrier(jnp.sum(remap_w, axis=1, keepdims=True))
    raw = jnp.einsum('tfk,tku->tfu', requested, normal, precision=lax.Precision.HIGHEST)
    return (raw, normal)

def remap_out(unit_fluxes, normal):
    tiles = normal.shape[0]
    contrib = jnp.einsum('tku,tfu->tfk', normal, unit_fluxes, precision=lax.Precision.HIGHEST)
    contrib = contrib.reshape(tiles, NFLUX, REF, GLL).transpose(0, 2, 1, 3)
    return contrib.reshape(tiles * REF, NFLUX * GLL)

def column_mixing(atm_state, mixing):
    state = atm_state
    for iteration in range(SUB):
        pieces = [jnp.dot(state[:, variable * LEV:(variable + 1) * LEV], mixing[variable], preferred_element_type=jnp.float32) for variable in range(NV)]
        update = jnp.concatenate(pieces, axis=1)
        state = (state.astype(jnp.float32) + 0.25 * jnp.tanh(update)).astype(jnp.bfloat16)
    return state

def finish(mixed, col_flux):
    result = mixed.astype(jnp.float32)
    result = result.at[:, 0].add(0.1 * col_flux[0]).at[:, LEV].add(0.1 * col_flux[6])
    return result.astype(jnp.bfloat16)

def reference(atm_state, profile, mixing, radiation, ocean_mask, tile_src, tile_elem, remap_w, slope_class, aspect_class, sky_view, albedo, sun_cos, sun_azimuth):
    elem_count = ELEM_DEV * N_SECT * N_LANE
    tiles = tile_src.shape[0]
    forcing = forcing_fields(atm_state, profile, radiation)
    blocks = forcing.reshape(NF, elem_count, GLL).transpose(1, 0, 2).reshape(elem_count, NF * GLL)
    element_ids = (tile_src * ELEM_DEV + tile_elem).reshape(-1).astype(jnp.int32)
    requested = blocks[element_ids].reshape(tiles, REF, NF, GLL).transpose(0, 2, 1, 3).reshape(tiles, NF, REF * GLL)
    raw, normal = remap_in(requested, remap_w)
    land_temp, unit_fluxes = land_balance(raw, sky_view, albedo, slope_class, aspect_class, sun_cos, sun_azimuth)
    contrib = remap_out(unit_fluxes, normal)
    land_part = jnp.zeros((elem_count, NFLUX * GLL), jnp.float32).at[element_ids].add(contrib)
    land_part = land_part.reshape(elem_count, NFLUX, GLL).transpose(1, 0, 2).reshape(NFLUX, elem_count * GLL)
    col_flux = land_part + ocean_mask.astype(jnp.float32) * ocean_fluxes(forcing)
    mixed = column_mixing(atm_state, mixing)
    return (finish(mixed, col_flux), land_temp, col_flux)
```

```python
import functools
import math

import jax
import jax.numpy as jnp
from jax import lax
from jax.experimental import pallas as pl
from jax.experimental.pallas import tpu as pltpu
from jax.sharding import PartitionSpec as P

GLL = 16
LEV = 128
NV = 4
NF = 8
SUB = 4
NEWTON = 2
NASPECT = 8
CAP = 16
UNIT = 128
REF = 4
KDIM = REF * GLL
AXES = ("sect", "lane")

F32 = jnp.float32
BF16 = jnp.bfloat16
I32 = jnp.int32
MIB = 1 << 20


def iota(shape, axis):
    return lax.broadcasted_iota(I32, shape, axis)


def matmul(left, right):
    return jnp.dot(left, right, preferred_element_type=F32)


def matmul_nt(left, right):
    return lax.dot_general(left, right, (((1,), (1,)), ((), ())), preferred_element_type=F32)


def flag(condition):
    return jnp.where(condition, 1.0, 0.0).astype(BF16)


def high_low(values):
    high = values.astype(BF16).astype(F32)
    return high, values - high


def pair(values):
    high, low = high_low(values)
    return jnp.concatenate([high.astype(BF16), low.astype(BF16)], axis=1)


def fold(values):
    half = values.shape[1] // 2
    return values[:, :half] + values[:, half:]


def block_swap(values):
    cube = values.reshape(values.shape[0] // 8, 8, 128)
    rows, lanes = iota(cube.shape, 1), iota(cube.shape, 2)
    for step in range(3):
        reach = 1 << step
        row_bit, chunk_bit = (rows >> step) & 1, (lanes >> (4 + step)) & 1
        up = pltpu.roll(pltpu.roll(cube, 8 - reach, 1), 16 * reach, 2)
        if reach == 4:
            moved = up
        else:
            down = pltpu.roll(pltpu.roll(cube, reach, 1), 128 - 16 * reach, 2)
            moved = jnp.where(chunk_bit == 1, up, down)
        cube = jnp.where(row_bit == chunk_bit, cube, moved)
    return cube.reshape(values.shape)


def drivers(fields):
    air_temp = 1.0 + 0.05 * jnp.tanh(fields[0])
    air_humid = 0.02 / (1.0 + jnp.exp(-fields[1]))
    wind_speed = jnp.sqrt(1.0 + fields[2] * fields[2] + fields[3] * fields[3])
    return (
        air_temp,
        air_humid,
        wind_speed,
        1.5 * fields[4],
        0.5 * fields[5],
        0.6 + 0.3 * fields[6],
        fields[7],
    )


def flux_list(surface, fields, driven, absorbed, reflected, wetness):
    air_temp, air_humid, wind_speed = driven[:3]
    heat_coef = 0.1 * wind_speed
    vapor_coef = 0.25 * wind_speed * wetness
    saturation = 0.02 * jnp.exp(17.0 * (surface - 1.0))
    sensible = heat_coef * (surface - air_temp)
    latent = vapor_coef * (saturation - air_humid)
    square = surface * surface
    upward = 0.95 * (square * square)
    drag = 0.05 * wind_speed
    return [
        sensible,
        latent,
        upward,
        reflected,
        drag * fields[2],
        drag * fields[3],
        0.4 * latent,
        absorbed - upward - sensible - latent,
    ]


def route_kernel(src_ref, elem_ref, want_ref, row_ref, col_ref):
    devices, tiles = want_ref.shape[0], src_ref.shape[1]
    owner = iota((devices, tiles), 0)
    slot = iota((128, tiles), 0)
    earlier = flag(iota((tiles, tiles), 0) < iota((tiles, tiles), 1))
    base = jnp.zeros((devices, 1), F32)
    wanted = jnp.zeros((devices, 128), F32)
    places = []
    for ref in range(REF):
        source = src_ref[ref : ref + 1, :]
        hit = owner == source
        onehot = flag(hit)
        before = matmul(onehot, earlier) + base
        rank = jnp.sum(jnp.where(hit, before, 0.0), axis=0, keepdims=True)
        base = base + jnp.sum(jnp.where(hit, 1.0, 0.0), axis=1, keepdims=True)
        rank = rank.astype(I32)
        value = (elem_ref[ref : ref + 1, :] + 1).astype(F32)
        table = jnp.where(slot == rank, value, 0.0).astype(BF16)
        wanted = wanted + matmul_nt(onehot, table)
        places.append(source * CAP + rank)
    want_ref[...] = wanted.astype(I32) - 1
    for ref in range(REF):
        row_ref[ref : ref + 1, :] = places[ref]
    stacked = jnp.concatenate(places + places, axis=0).astype(F32)
    col_ref[...] = jnp.transpose(stacked).astype(I32)


def forcing_kernel(profile_ref, state_ref, radiation_ref, forcing_ref, blocks_ref):
    whole = profile_ref[...]
    first = whole.astype(BF16).astype(F32)
    second = (whole - first).astype(BF16).astype(F32)
    third = whole - first - second
    rows = iota((32, LEV), 0)
    piece = jnp.where(rows < 8, first, jnp.where(rows < 16, second, jnp.where(rows < 24, third, 0.0)))
    spread = jnp.concatenate(
        [jnp.where((rows & 7) == variable, piece, 0.0) for variable in range(NV)], axis=1
    ).astype(BF16)
    sums = matmul_nt(spread, state_ref[...])
    means = sums[0:8] + sums[8:16] + sums[16:24]
    forcing = jnp.concatenate([means[0:NV], radiation_ref[...]], axis=0)
    forcing_ref[...] = forcing
    columns = forcing.shape[1]
    stacked = jnp.concatenate(
        [forcing[:, start : start + 128] for start in range(0, columns, 128)], axis=0
    )
    blocks_ref[...] = pair(block_swap(stacked))


def reply_kernel(incoming_ref, blocks_ref, reply_ref):
    devices, elements = incoming_ref.shape[0], blocks_ref.shape[0]
    element = iota((devices, elements), 1)
    blocks = blocks_ref[...]
    incoming = incoming_ref[...]
    for slot in range(CAP):
        select = flag(element == incoming[:, slot : slot + 1])
        reply_ref[pl.ds(slot, devices, stride=CAP), :] = fold(matmul(select, blocks))


def mix_kernel(mixing_ref, state_ref, mixed_ref):
    zero = jnp.zeros((LEV, LEV), BF16)
    operator = jnp.concatenate(
        [
            jnp.concatenate([mixing_ref[0], zero], axis=1),
            jnp.concatenate([zero, mixing_ref[1]], axis=1),
        ],
        axis=0,
    )
    rows = state_ref.shape[0]
    part = 256
    for start in range(0, rows, part):
        state = state_ref[start : start + part, :]
        for iteration in range(SUB):
            update = matmul(state, operator)
            state = (state.astype(F32) + 0.25 * jnp.tanh(update)).astype(BF16)
        mixed_ref[start : start + part, :] = state


def ocean_kernel(forcing_ref, mask_ref, ocean_ref):
    fields = [forcing_ref[index : index + 1, :] for index in range(NF)]
    driven = drivers(fields)
    shortwave = driven[3] + driven[4]
    absorbed = 0.94 * shortwave + 0.95 * driven[5]
    one = jnp.ones_like(fields[0])
    fluxes = flux_list(one, fields, driven, absorbed, 0.06 * shortwave, one)
    mask = mask_ref[...].astype(F32)
    for index in range(NF):
        ocean_ref[index : index + 1, :] = mask * fluxes[index]


def land_kernel(
    arrived_ref,
    row_ref,
    col_ref,
    w_ref,
    incidence_ref,
    sky_ref,
    albedo_ref,
    temp_ref,
    outgoing_ref,
    need_ref,
    both_ref,
    raw_ref,
    total_ref,
):
    step = pl.program_id(0)
    slots = arrived_ref.shape[0]
    tiles = row_ref.shape[1]
    step_tiles = w_ref.shape[0] // KDIM
    groups = step_tiles // 4

    @pl.when(step == 0)
    def _():
        arrived = pair(arrived_ref[...])
        slot = iota((tiles, slots), 1)
        for ref in range(REF):
            pick = flag(slot == col_ref[:, ref : ref + 1])
            need_ref[pl.ds(ref, tiles, stride=REF), :] = fold(matmul(pick, arrived))
        need_ref[...] = block_swap(need_ref[...])

    left = iota((8, 128), 1) < KDIM
    zero = jnp.zeros((8, 128), F32)
    lane = iota((16, 256), 1)
    ones = jnp.where((lane >> 6) == iota((16, 256), 0), 1.0, 0.0)

    for group in range(groups):
        weights = pair(w_ref[group * 256 : (group + 1) * 256, :])
        both_ref[pl.ds(pl.multiple_of(step * (groups * 256), 256) + group * 256, 256), :] = weights
        start = pl.multiple_of(step * (groups * 16), 16) + group * 16
        need = need_ref[pl.ds(start, 16), :]
        rows = []
        for part in high_low(need):
            for half in range(2):
                block = part[half * 8 : half * 8 + 8]
                for masked in (jnp.where(left, block, 0.0), jnp.where(left, 0.0, block)):
                    rows.append(
                        jnp.concatenate([masked, zero] if half == 0 else [zero, masked], axis=1)
                    )
        rows.append(ones)
        product = fold(matmul(jnp.concatenate(rows, axis=0).astype(BF16), weights))
        raw_ref[pl.ds(pl.multiple_of(step * (groups * 32), 32) + group * 32, 32), :] = (
            product[0:32] + product[32:64]
        )
        total_ref[pl.ds(pl.multiple_of(step * (groups * 8), 8) + group * 8, 8), :] = product[64:72]

    @pl.when(step == pl.num_programs(0) - 1)
    def _():
        sums = jnp.concatenate(
            [
                total_ref[index * 8 : index * 8 + 4, :]
                for index in range(tiles // 4)
            ],
            axis=0,
        )
        inverse = 1.0 / sums
        fields = [raw_ref[pl.ds(index, tiles, stride=NF), :] * inverse for index in range(NF)]
        driven = drivers(fields)
        air_temp, air_humid, wind_speed, direct_sw, diffuse_sw, longwave, wetness = driven
        sky, albedo = sky_ref[...], albedo_ref[...]
        shortwave = direct_sw * incidence_ref[...] + diffuse_sw * sky
        absorbed = (1.0 - albedo) * shortwave + 0.95 * longwave * sky
        heat_coef = 0.1 * wind_speed
        vapor_coef = 0.25 * wind_speed * wetness
        surface = air_temp
        for iteration in range(NEWTON):
            saturation = 0.02 * jnp.exp(17.0 * (surface - 1.0))
            square = surface * surface
            imbalance = (
                absorbed
                - 0.95 * (square * square)
                - heat_coef * (surface - air_temp)
                - vapor_coef * (saturation - air_humid)
            )
            derivative = -3.8 * (square * surface) - heat_coef - 17.0 * vapor_coef * saturation
            surface = surface - imbalance / derivative
        temp_ref[...] = surface
        fluxes = flux_list(surface, fields, driven, absorbed, albedo * shortwave, wetness)
        for index in range(NF):
            raw_ref[pl.ds(index, tiles, stride=NF), :] = fluxes[index] * inverse

        def give(group, carry):
            flux = raw_ref[pl.ds(pl.multiple_of(group * 32, 32), 32), :]
            high, low = high_low(flux)
            stacked = jnp.concatenate([high, low], axis=0).astype(BF16)
            stacked = jnp.concatenate([stacked, stacked], axis=1)
            weights = both_ref[pl.ds(pl.multiple_of(group * 256, 256), 256), :]
            product = matmul_nt(stacked, weights)
            product = product[0:32] + product[32:64]
            need_ref[pl.ds(pl.multiple_of(group * 16, 16), 16), :] = jnp.concatenate(
                [
                    jnp.where(left, product[0:8, 0:128], product[8:16, 0:128]),
                    jnp.where(left, product[16:24, 128:256], product[24:32, 128:256]),
                ],
                axis=0,
            )
            return carry

        lax.fori_loop(0, tiles // 4, give, 0, unroll=8)
        need_ref[...] = block_swap(need_ref[...])
        given = jnp.concatenate(
            [pair(need_ref[pl.ds(ref, tiles, stride=REF), :]) for ref in range(REF)], axis=0
        )
        size = 256

        def place(index, carry):
            start = pl.multiple_of(index * size, size)
            slot = iota((size, tiles), 0) + start
            pick = jnp.concatenate(
                [flag(slot == row_ref[ref : ref + 1, :]) for ref in range(REF)], axis=1
            )
            outgoing_ref[pl.ds(start, size), :] = fold(matmul(pick, given))
            return carry

        lax.fori_loop(0, slots // size, place, 0, unroll=2)


def finish_kernel(returned_ref, incoming_ref, ocean_ref, mixed_ref, kept_ref, out_ref, flux_ref):
    del kept_ref
    step = pl.program_id(0)
    devices = incoming_ref.shape[0]
    elements = flux_ref.shape[1] // GLL

    @pl.when(step == 0)
    def _():
        incoming = jnp.transpose(incoming_ref[...].astype(F32)).astype(I32)
        element = iota((elements, devices), 0)
        part = jnp.zeros((elements, 256), F32)
        for slot in range(0, CAP, 2):
            select = jnp.concatenate(
                [flag(element == incoming[slot + extra : slot + extra + 1, :]) for extra in range(2)],
                axis=1,
            )
            values = jnp.concatenate(
                [
                    pair(returned_ref[pl.ds(slot + extra, devices, stride=CAP), :])
                    for extra in range(2)
                ],
                axis=0,
            )
            part = part + matmul(select, values)
        swapped = block_swap(fold(part))
        for index in range(elements // 8):
            columns = slice(index * 128, index * 128 + 128)
            flux_ref[:, columns] = swapped[index * 8 : index * 8 + 8] + ocean_ref[:, columns]

    rows = out_ref.shape[0]
    lane = iota((128, 128), 1)
    for start in range(0, rows, 128):
        begin = pl.multiple_of(step * rows, rows) + start
        turned = jnp.transpose(flux_ref[:, pl.ds(begin, 128)])
        for half, index in ((0, 0), (1, 6)):
            lanes = slice(half * 128, half * 128 + 128)
            added = jnp.where(lane == 0, 0.1 * turned[:, index : index + 1], 0.0)
            state = mixed_ref[start : start + 128, lanes].astype(F32)
            out_ref[start : start + 128, lanes] = (state + added).astype(BF16)


def whole(*shape):
    return pl.BlockSpec(shape, lambda *_: (0,) * len(shape))


def params(mebibytes, axes=0):
    return pltpu.CompilerParams(
        vmem_limit_bytes=mebibytes * MIB,
        dimension_semantics=("arbitrary",) * axes if axes else None,
    )


def cost(flops, moved, hard=0):
    return pl.CostEstimate(flops=int(flops), bytes_accessed=int(moved), transcendentals=int(hard))


def mix(mixing, atm_state, half, place_half, width):
    columns = atm_state.shape[0]
    rows = 512
    return pl.pallas_call(
        mix_kernel,
        grid=(columns // rows,),
        in_specs=[
            pl.BlockSpec((2, LEV, LEV), lambda i: (half, 0, 0)),
            pl.BlockSpec((rows, 256), lambda i: (i, half)),
        ],
        out_specs=pl.BlockSpec((rows, 256), lambda i: (i, place_half)),
        out_shape=jax.ShapeDtypeStruct((columns, width), BF16),
        compiler_params=params(16, 1),
        cost_estimate=cost(columns * 256 * 256 * 2 * SUB, columns * 256 * 4, columns * 256 * SUB),
    )(mixing, atm_state)


def on_device(
    atm_state,
    profile,
    mixing,
    radiation,
    ocean_mask,
    tile_src,
    tile_elem,
    remap_w,
    slope_class,
    aspect_class,
    sky_view,
    albedo,
    sun_cos,
    sun_azimuth,
):
    devices = lax.axis_size("sect") * lax.axis_size("lane")
    columns = atm_state.shape[0]
    elements = columns // GLL
    tiles = tile_src.shape[0]
    slots = devices * CAP
    requests = tiles * REF

    wanted, slot_row, slot_col = pl.pallas_call(
        route_kernel,
        out_shape=(
            jax.ShapeDtypeStruct((devices, 128), I32),
            jax.ShapeDtypeStruct((REF, tiles), I32),
            jax.ShapeDtypeStruct((tiles, 2 * REF), I32),
        ),
        compiler_params=params(16),
    )(tile_src.T, tile_elem.T)
    incoming = lax.all_to_all(wanted, AXES, split_axis=0, concat_axis=0, tiled=True)

    rows = 512
    forcing, blocks = pl.pallas_call(
        forcing_kernel,
        grid=(columns // rows,),
        in_specs=[
            whole(1, LEV),
            pl.BlockSpec((rows, NV * LEV), lambda i: (i, 0)),
            pl.BlockSpec((4, rows), lambda i: (0, i)),
        ],
        out_specs=(
            pl.BlockSpec((NF, rows), lambda i: (0, i)),
            pl.BlockSpec((rows // GLL, 256), lambda i: (i, 0)),
        ),
        out_shape=(
            jax.ShapeDtypeStruct((NF, columns), F32),
            jax.ShapeDtypeStruct((elements, 256), BF16),
        ),
        compiler_params=params(16, 1),
        cost_estimate=cost(columns * 512 * 32 * 2, columns * 1024),
    )(profile.reshape(1, LEV), atm_state, radiation)

    reply = pl.pallas_call(
        reply_kernel,
        out_shape=jax.ShapeDtypeStruct((slots, 128), F32),
        compiler_params=params(16),
        cost_estimate=cost(slots * 256 * 256 * 2, slots * 512),
    )(incoming, blocks)
    arrived = lax.all_to_all(
        reply.reshape(devices, CAP, 128), AXES, split_axis=0, concat_axis=0, tiled=True
    ).reshape(slots, 128)

    kept = mix(mixing, atm_state, 1, 1, NV * LEV)
    cosine = sun_cos[:, None]
    sine = jnp.sqrt(1.0 - cosine * cosine)
    slope_angle = slope_class.astype(F32) * 0.1
    aspect_angle = aspect_class.astype(F32) * (2.0 * math.pi / NASPECT)
    incidence = (
        jnp.maximum(
            0.0,
            jnp.cos(slope_angle) * cosine
            + jnp.sin(slope_angle) * sine * jnp.cos(sun_azimuth[:, None] - aspect_angle),
        )
        / cosine
    )

    step_tiles = 32
    land_temp, outgoing = pl.pallas_call(
        land_kernel,
        grid=(tiles // step_tiles,),
        in_specs=[
            whole(slots, 128),
            whole(REF, tiles),
            whole(tiles, 2 * REF),
            pl.BlockSpec((step_tiles * KDIM, UNIT), lambda i: (i, 0)),
            whole(tiles, UNIT),
            whole(tiles, UNIT),
            whole(tiles, UNIT),
        ],
        out_specs=(whole(tiles, UNIT), whole(slots, 128)),
        out_shape=(
            jax.ShapeDtypeStruct((tiles, UNIT), F32),
            jax.ShapeDtypeStruct((slots, 128), F32),
        ),
        scratch_shapes=[
            pltpu.VMEM((requests, 128), F32),
            pltpu.VMEM((tiles * KDIM, 256), BF16),
            pltpu.VMEM((tiles * NF, 128), F32),
            pltpu.VMEM((tiles * 2, 128), F32),
        ],
        compiler_params=params(40, 1),
        cost_estimate=cost(4 * requests * slots * 256 * 2, tiles * KDIM * UNIT * 4),
    )(
        arrived,
        slot_row,
        slot_col,
        remap_w.reshape(tiles * KDIM, UNIT),
        incidence,
        sky_view,
        albedo,
    )
    returned = lax.all_to_all(
        outgoing.reshape(devices, CAP, 128), AXES, split_axis=0, concat_axis=0, tiled=True
    ).reshape(slots, 128)

    mixed = mix(mixing, atm_state, 0, 0, 2 * LEV)
    ocean = pl.pallas_call(
        ocean_kernel,
        out_shape=jax.ShapeDtypeStruct((NF, columns), F32),
        compiler_params=params(16),
        cost_estimate=cost(columns * 100, columns * 64, columns * 4),
    )(forcing, ocean_mask.reshape(1, columns))

    rows = 1024
    atm_out, col_flux = pl.pallas_call(
        finish_kernel,
        grid=(columns // rows,),
        in_specs=[
            whole(slots, 128),
            whole(devices, 128),
            whole(NF, columns),
            pl.BlockSpec((rows, 256), lambda i: (i, 0)),
            pl.BlockSpec(memory_space=pl.ANY),
        ],
        out_specs=(
            pl.BlockSpec((rows, 256), lambda i: (i, 0)),
            whole(NF, columns),
        ),
        out_shape=(
            jax.ShapeDtypeStruct((columns, NV * LEV), BF16),
            jax.ShapeDtypeStruct((NF, columns), F32),
        ),
        input_output_aliases={4: 0},
        compiler_params=params(16, 1),
    )(returned, incoming, ocean, mixed, kept)
    return (atm_out, land_temp, col_flux)


def solution(mesh):
    return jax.shard_map(
        on_device,
        mesh=mesh,
        in_specs=(
            P(AXES, None),
            P(),
            P(),
            P(None, AXES),
            P(AXES),
            P(AXES, None),
            P(AXES, None),
            P(AXES, None, None),
            P(AXES, None),
            P(AXES, None),
            P(AXES, None),
            P(AXES, None),
            P(AXES),
            P(AXES),
        ),
        out_specs=(P(AXES, None), P(AXES, None), P(None, AXES)),
        check_vma=False,
    )
```

```python
import functools
import math

import jax
import jax.numpy as jnp
from jax import lax
from jax.experimental import pallas as pl
from jax.experimental.pallas import tpu as pltpu
from jax.sharding import PartitionSpec as P

GLL = 16
LEV = 128
NV = 4
NF = 8
SUB = 4
NEWTON = 2
NASPECT = 8
CAP = 16
UNIT = 128
REF = 4
KDIM = REF * GLL
AXES = ("sect", "lane")

F32 = jnp.float32
BF16 = jnp.bfloat16
I32 = jnp.int32
MIB = 1 << 20


def iota(shape, axis):
    return lax.broadcasted_iota(I32, shape, axis)


def matmul(left, right):
    return jnp.dot(left, right, preferred_element_type=F32)


def matmul_nt(left, right):
    return lax.dot_general(left, right, (((1,), (1,)), ((), ())), preferred_element_type=F32)


def flag(condition):
    return jnp.where(condition, 1.0, 0.0).astype(BF16)


def high_low(values):
    high = values.astype(BF16).astype(F32)
    return high, values - high


def pair(values):
    high, low = high_low(values)
    return jnp.concatenate([high.astype(BF16), low.astype(BF16)], axis=1)


def fold(values):
    half = values.shape[1] // 2
    return values[:, :half] + values[:, half:]


def block_swap(values):
    cube = values.reshape(values.shape[0] // 8, 8, 128)
    rows, lanes = iota(cube.shape, 1), iota(cube.shape, 2)
    for step in range(3):
        reach = 1 << step
        row_bit, chunk_bit = (rows >> step) & 1, (lanes >> (4 + step)) & 1
        up = pltpu.roll(pltpu.roll(cube, 8 - reach, 1), 16 * reach, 2)
        if reach == 4:
            moved = up
        else:
            down = pltpu.roll(pltpu.roll(cube, reach, 1), 128 - 16 * reach, 2)
            moved = jnp.where(chunk_bit == 1, up, down)
        cube = jnp.where(row_bit == chunk_bit, cube, moved)
    return cube.reshape(values.shape)


def drivers(fields):
    air_temp = 1.0 + 0.05 * jnp.tanh(fields[0])
    air_humid = 0.02 / (1.0 + jnp.exp(-fields[1]))
    wind_speed = jnp.sqrt(1.0 + fields[2] * fields[2] + fields[3] * fields[3])
    return (
        air_temp,
        air_humid,
        wind_speed,
        1.5 * fields[4],
        0.5 * fields[5],
        0.6 + 0.3 * fields[6],
        fields[7],
    )


def flux_list(surface, fields, driven, absorbed, reflected, wetness):
    air_temp, air_humid, wind_speed = driven[:3]
    heat_coef = 0.1 * wind_speed
    vapor_coef = 0.25 * wind_speed * wetness
    saturation = 0.02 * jnp.exp(17.0 * (surface - 1.0))
    sensible = heat_coef * (surface - air_temp)
    latent = vapor_coef * (saturation - air_humid)
    square = surface * surface
    upward = 0.95 * (square * square)
    drag = 0.05 * wind_speed
    return [
        sensible,
        latent,
        upward,
        reflected,
        drag * fields[2],
        drag * fields[3],
        0.4 * latent,
        absorbed - upward - sensible - latent,
    ]


def start_copies(source, target, sems, parts):
    rows = target.shape[0] // parts
    copies = []
    for part in range(parts):
        span = pl.ds(part * rows, rows)
        copy = pltpu.make_async_copy(source.at[span, :], target.at[span, :], sems.at[part])
        copy.start()
        copies.append(copy)
    return copies


def route_kernel(src_ref, elem_ref, want_ref, row_ref, col_ref):
    devices, tiles = want_ref.shape[0], src_ref.shape[1]
    owner = iota((devices, tiles), 0)
    slot = iota((128, tiles), 0)
    earlier = flag(iota((tiles, tiles), 0) < iota((tiles, tiles), 1))
    base = jnp.zeros((devices, 1), F32)
    wanted = jnp.zeros((devices, 128), F32)
    places = []
    for ref in range(REF):
        source = src_ref[ref : ref + 1, :]
        hit = owner == source
        onehot = flag(hit)
        before = matmul(onehot, earlier) + base
        rank = jnp.sum(jnp.where(hit, before, 0.0), axis=0, keepdims=True)
        base = base + jnp.sum(jnp.where(hit, 1.0, 0.0), axis=1, keepdims=True)
        rank = rank.astype(I32)
        value = (elem_ref[ref : ref + 1, :] + 1).astype(F32)
        table = jnp.where(slot == rank, value, 0.0).astype(BF16)
        wanted = wanted + matmul_nt(onehot, table)
        places.append(source * CAP + rank)
    want_ref[...] = wanted.astype(I32) - 1
    for ref in range(REF):
        row_ref[ref : ref + 1, :] = places[ref]
    stacked = jnp.concatenate(places + places, axis=0).astype(F32)
    col_ref[...] = jnp.transpose(stacked).astype(I32)


def forcing_kernel(
    profile_ref,
    state_ref,
    radiation_ref,
    forcing_ref,
    blocks_ref,
    held_ref,
    sems,
):
    parts = sems.shape[0]
    copies = start_copies(state_ref, held_ref, sems, parts)
    profile = profile_ref[...]
    first = profile.astype(BF16).astype(F32)
    second = (profile - first).astype(BF16).astype(F32)
    third = profile - first - second
    rows = iota((32, LEV), 0)
    piece = jnp.where(rows < 8, first, jnp.where(rows < 16, second, jnp.where(rows < 24, third, 0.0)))
    spread = jnp.concatenate(
        [jnp.where((rows & 7) == variable, piece, 0.0) for variable in range(NV)], axis=1
    ).astype(BF16)
    size = held_ref.shape[0] // parts
    pieces = []
    for part in range(parts):
        copies[part].wait()
        columns = slice(part * size, part * size + size)
        sums = matmul_nt(spread, held_ref[columns, :])
        means = sums[0:8] + sums[8:16] + sums[16:24]
        forcing = jnp.concatenate([means[0:NV], radiation_ref[:, columns]], axis=0)
        forcing_ref[:, columns] = forcing
        pieces += [forcing[:, start : start + 128] for start in range(0, size, 128)]
    blocks_ref[...] = pair(block_swap(jnp.concatenate(pieces, axis=0)))


def reply_kernel(incoming_ref, blocks_ref, reply_ref):
    devices, elements = incoming_ref.shape[0], blocks_ref.shape[0]
    element = iota((devices, elements), 1)
    blocks = blocks_ref[...]
    incoming = incoming_ref[...]
    for slot in range(CAP):
        select = flag(element == incoming[:, slot : slot + 1])
        reply_ref[pl.ds(slot, devices, stride=CAP), :] = fold(matmul(select, blocks))


def prepare_kernel(w_ref, both_ref, inverse_ref):
    rows = w_ref.shape[0]
    part = 1024
    for start in range(0, rows, part):
        weights = w_ref[start : start + part, :]
        both_ref[start : start + part, :] = pair(weights)
        total = jnp.sum(weights.reshape(part // KDIM, KDIM, UNIT), axis=1)
        inverse_ref[start // KDIM : (start + part) // KDIM, :] = 1.0 / total


def mix_rows(mixing_ref, held_ref, size, done):
    zero = jnp.zeros((LEV, LEV), BF16)
    operator = jnp.concatenate(
        [
            jnp.concatenate([mixing_ref[0], zero], axis=1),
            jnp.concatenate([zero, mixing_ref[1]], axis=1),
        ],
        axis=0,
    )

    def work(part, carry):
        done(part, None)
        span = pl.ds(pl.multiple_of(part * size, size), size)
        state = held_ref[span, :]
        for iteration in range(SUB):
            update = matmul(state, operator)
            state = (state.astype(F32) + 0.25 * jnp.tanh(update)).astype(BF16)
        done(part, state)
        return carry

    lax.fori_loop(0, held_ref.shape[0] // size, work, 0)


def mix_kernel(half, out_half, mixing_ref, state_ref, mixed_ref, held_ref, into, out):
    parts = into.shape[0]
    size = held_ref.shape[0] // parts
    lanes = pl.ds(half * 256, 256)

    def copy_in(part):
        span = pl.ds(pl.multiple_of(part * size, size), size)
        return pltpu.make_async_copy(state_ref.at[span, lanes], held_ref.at[span, :], into.at[part])

    def copy_out(part):
        span = pl.ds(pl.multiple_of(part * size, size), size)
        return pltpu.make_async_copy(
            held_ref.at[span, :], mixed_ref.at[span, pl.ds(out_half * 256, 256)], out.at[part]
        )

    for part in range(parts):
        copy_in(part).start()

    def done(part, state):
        if state is None:
            copy_in(part).wait()
            return
        span = pl.ds(pl.multiple_of(part * size, size), size)
        if out_half is None:
            mixed_ref[span, :] = state
        else:
            held_ref[span, :] = state
            copy_out(part).start()

    mix_rows(mixing_ref, held_ref, size, done)
    if out_half is not None:
        for part in range(parts):
            copy_out(part).wait()


def ocean_kernel(forcing_ref, mask_ref, ocean_ref):
    fields = [forcing_ref[index : index + 1, :] for index in range(NF)]
    driven = drivers(fields)
    shortwave = driven[3] + driven[4]
    absorbed = 0.94 * shortwave + 0.95 * driven[5]
    one = jnp.ones_like(fields[0])
    fluxes = flux_list(one, fields, driven, absorbed, 0.06 * shortwave, one)
    mask = mask_ref[...].astype(F32)
    for index in range(NF):
        ocean_ref[index : index + 1, :] = mask * fluxes[index]


def land_kernel(
    arrived_ref,
    row_ref,
    col_ref,
    both_ref,
    inverse_ref,
    incidence_ref,
    sky_ref,
    albedo_ref,
    temp_ref,
    outgoing_ref,
    need_ref,
    raw_ref,
    held_ref,
    sems,
):
    slots = arrived_ref.shape[0]
    tiles = row_ref.shape[1]
    parts = sems.shape[0]
    copies = start_copies(both_ref, held_ref, sems, parts)
    arrived = pair(arrived_ref[...])
    slot = iota((tiles, slots), 1)
    for ref in range(REF):
        pick = flag(slot == col_ref[:, ref : ref + 1])
        need_ref[pl.ds(ref, tiles, stride=REF), :] = fold(matmul(pick, arrived))
    need_ref[...] = block_swap(need_ref[...])

    left = iota((8, 128), 1) < KDIM
    zero = jnp.zeros((8, 128), F32)

    def take(group, carry):
        weights = held_ref[pl.ds(pl.multiple_of(group * 256, 256), 256), :]
        need = need_ref[pl.ds(pl.multiple_of(group * 16, 16), 16), :]
        rows = []
        for part in high_low(need):
            for half in range(2):
                block = part[half * 8 : half * 8 + 8]
                for masked in (jnp.where(left, block, 0.0), jnp.where(left, 0.0, block)):
                    rows.append(
                        jnp.concatenate([masked, zero] if half == 0 else [zero, masked], axis=1)
                    )
        product = fold(matmul(jnp.concatenate(rows, axis=0).astype(BF16), weights))
        raw_ref[pl.ds(pl.multiple_of(group * 32, 32), 32), :] = product[0:32] + product[32:64]
        return carry

    size = tiles // 4 // parts
    for part in range(parts):
        copies[part].wait()
        lax.fori_loop(part * size, (part + 1) * size, take, 0, unroll=8)

    inverse = inverse_ref[...]
    fields = [raw_ref[pl.ds(index, tiles, stride=NF), :] * inverse for index in range(NF)]
    driven = drivers(fields)
    air_temp, air_humid, wind_speed, direct_sw, diffuse_sw, longwave, wetness = driven
    sky, albedo = sky_ref[...], albedo_ref[...]
    shortwave = direct_sw * incidence_ref[...] + diffuse_sw * sky
    absorbed = (1.0 - albedo) * shortwave + 0.95 * longwave * sky
    heat_coef = 0.1 * wind_speed
    vapor_coef = 0.25 * wind_speed * wetness
    surface = air_temp
    for iteration in range(NEWTON):
        saturation = 0.02 * jnp.exp(17.0 * (surface - 1.0))
        square = surface * surface
        imbalance = (
            absorbed
            - 0.95 * (square * square)
            - heat_coef * (surface - air_temp)
            - vapor_coef * (saturation - air_humid)
        )
        derivative = -3.8 * (square * surface) - heat_coef - 17.0 * vapor_coef * saturation
        surface = surface - imbalance / derivative
    temp_ref[...] = surface
    fluxes = flux_list(surface, fields, driven, absorbed, albedo * shortwave, wetness)
    for index in range(NF):
        raw_ref[pl.ds(index, tiles, stride=NF), :] = fluxes[index] * inverse

    def give(group, carry):
        flux = raw_ref[pl.ds(pl.multiple_of(group * 32, 32), 32), :]
        high, low = high_low(flux)
        stacked = jnp.concatenate([high, low], axis=0).astype(BF16)
        stacked = jnp.concatenate([stacked, stacked], axis=1)
        weights = held_ref[pl.ds(pl.multiple_of(group * 256, 256), 256), :]
        product = matmul_nt(stacked, weights)
        product = product[0:32] + product[32:64]
        need_ref[pl.ds(pl.multiple_of(group * 16, 16), 16), :] = jnp.concatenate(
            [
                jnp.where(left, product[0:8, 0:128], product[8:16, 0:128]),
                jnp.where(left, product[16:24, 128:256], product[24:32, 128:256]),
            ],
            axis=0,
        )
        return carry

    lax.fori_loop(0, tiles // 4, give, 0, unroll=16)
    need_ref[...] = block_swap(need_ref[...])
    given = jnp.concatenate(
        [pair(need_ref[pl.ds(ref, tiles, stride=REF), :]) for ref in range(REF)], axis=0
    )
    size = 256

    def place(index, carry):
        start = pl.multiple_of(index * size, size)
        spot = iota((size, tiles), 0) + start
        pick = jnp.concatenate(
            [flag(spot == row_ref[ref : ref + 1, :]) for ref in range(REF)], axis=1
        )
        outgoing_ref[pl.ds(start, size), :] = fold(matmul(pick, given))
        return carry

    lax.fori_loop(0, slots // size, place, 0, unroll=4)


def finish_kernel(
    returned_ref, incoming_ref, ocean_ref, mixed_ref, kept_ref, out_ref, flux_ref, held_ref, sems
):
    del kept_ref
    devices = incoming_ref.shape[0]
    elements = flux_ref.shape[1] // GLL
    incoming = jnp.transpose(incoming_ref[...].astype(F32)).astype(I32)
    element = iota((elements, devices), 0)
    part = jnp.zeros((elements, 256), F32)
    for slot in range(0, CAP, 2):
        select = jnp.concatenate(
            [flag(element == incoming[slot + extra : slot + extra + 1, :]) for extra in range(2)],
            axis=1,
        )
        values = jnp.concatenate(
            [pair(returned_ref[pl.ds(slot + extra, devices, stride=CAP), :]) for extra in range(2)],
            axis=0,
        )
        part = part + matmul(select, values)
    swapped = block_swap(fold(part))
    parts = sems.shape[0]
    size = held_ref.shape[0] // parts
    lane = iota((128, 128), 1)
    copies = []
    for index in range(parts):
        for start in range(index * size, index * size + size, 128):
            columns = slice(start, start + 128)
            flux = swapped[start // 16 : start // 16 + 8] + ocean_ref[:, columns]
            flux_ref[:, columns] = flux
            turned = jnp.transpose(flux)
            for half, row in ((0, 0), (1, 6)):
                lanes = slice(half * 128, half * 128 + 128)
                added = jnp.where(lane == 0, 0.1 * turned[:, row : row + 1], 0.0)
                state = mixed_ref[columns, lanes].astype(F32)
                held_ref[columns, lanes] = (state + added).astype(BF16)
        span = pl.ds(index * size, size)
        copy = pltpu.make_async_copy(
            held_ref.at[span, :], out_ref.at[span, pl.ds(0, 256)], sems.at[index]
        )
        copy.start()
        copies.append(copy)
    for copy in copies:
        copy.wait()


def whole(*shape):
    return pl.BlockSpec(shape, lambda *_: (0,) * len(shape))


def params(mebibytes, axes=0):
    return pltpu.CompilerParams(
        vmem_limit_bytes=mebibytes * MIB,
        dimension_semantics=("arbitrary",) * axes if axes else None,
    )


def cost(flops, moved, hard=0):
    return pl.CostEstimate(flops=int(flops), bytes_accessed=int(moved), transcendentals=int(hard))


def mix(mixing, atm_state, half, out_half):
    columns = atm_state.shape[0]
    parts = 4
    apart = out_half is None
    return pl.pallas_call(
        functools.partial(mix_kernel, half, out_half),
        grid=(1,),
        in_specs=[
            pl.BlockSpec((2, LEV, LEV), lambda i: (half, 0, 0)),
            pl.BlockSpec(memory_space=pltpu.HBM),
        ],
        out_specs=whole(columns, 256) if apart else pl.BlockSpec(memory_space=pltpu.HBM),
        out_shape=jax.ShapeDtypeStruct((columns, 256 if apart else NV * LEV), BF16),
        scratch_shapes=[
            pltpu.VMEM((columns, 256), BF16),
            pltpu.SemaphoreType.DMA((parts,)),
            pltpu.SemaphoreType.DMA((parts,)),
        ],
        compiler_params=params(16, 1),
        cost_estimate=cost(columns * 256 * 256 * 2 * SUB, columns * 256 * 4, columns * 256 * SUB),
    )(mixing, atm_state)


def on_device(
    atm_state,
    profile,
    mixing,
    radiation,
    ocean_mask,
    tile_src,
    tile_elem,
    remap_w,
    slope_class,
    aspect_class,
    sky_view,
    albedo,
    sun_cos,
    sun_azimuth,
):
    devices = lax.axis_size("sect") * lax.axis_size("lane")
    columns = atm_state.shape[0]
    elements = columns // GLL
    tiles = tile_src.shape[0]
    slots = devices * CAP
    requests = tiles * REF

    wanted, slot_row, slot_col = pl.pallas_call(
        route_kernel,
        out_shape=(
            jax.ShapeDtypeStruct((devices, 128), I32),
            jax.ShapeDtypeStruct((REF, tiles), I32),
            jax.ShapeDtypeStruct((tiles, 2 * REF), I32),
        ),
        compiler_params=params(60),
    )(tile_src.T, tile_elem.T)
    wanted, atm_state = lax.optimization_barrier((wanted, atm_state))
    incoming = lax.all_to_all(wanted, AXES, split_axis=0, concat_axis=0, tiled=True)

    parts = 4
    forcing, blocks = pl.pallas_call(
        forcing_kernel,
        grid=(1,),
        in_specs=[
            whole(1, LEV),
            pl.BlockSpec(memory_space=pltpu.HBM),
            whole(4, columns),
        ],
        out_specs=(whole(NF, columns), whole(elements, 256)),
        out_shape=(
            jax.ShapeDtypeStruct((NF, columns), F32),
            jax.ShapeDtypeStruct((elements, 256), BF16),
        ),
        scratch_shapes=[
            pltpu.VMEM((columns, NV * LEV), BF16),
            pltpu.SemaphoreType.DMA((parts,)),
        ],
        compiler_params=params(50, 1),
        cost_estimate=cost(columns * 512 * 32 * 2, columns * 1024),
    )(profile.reshape(1, LEV), atm_state, radiation)
    incoming, forcing, blocks = lax.optimization_barrier((incoming, forcing, blocks))

    reply = pl.pallas_call(
        reply_kernel,
        out_shape=jax.ShapeDtypeStruct((slots, 128), F32),
        compiler_params=params(16),
        cost_estimate=cost(slots * 256 * 256 * 2, slots * 512),
    )(incoming, blocks)
    reply, atm_state, remap_w, slope_class, sun_cos = lax.optimization_barrier(
        (reply, atm_state, remap_w, slope_class, sun_cos)
    )
    arrived = lax.all_to_all(
        reply.reshape(devices, CAP, 128), AXES, split_axis=0, concat_axis=0, tiled=True
    ).reshape(slots, 128)

    kept = mix(mixing, atm_state, 1, 1)
    cosine = sun_cos[:, None]
    sine = jnp.sqrt(1.0 - cosine * cosine)
    slope_angle = slope_class.astype(F32) * 0.1
    aspect_angle = aspect_class.astype(F32) * (2.0 * math.pi / NASPECT)
    incidence = (
        jnp.maximum(
            0.0,
            jnp.cos(slope_angle) * cosine
            + jnp.sin(slope_angle) * sine * jnp.cos(sun_azimuth[:, None] - aspect_angle),
        )
        / cosine
    )
    remap_w, kept, incidence = lax.optimization_barrier((remap_w, kept, incidence))
    rows = 4096
    both, inverse = pl.pallas_call(
        prepare_kernel,
        grid=(tiles * KDIM // rows,),
        in_specs=[pl.BlockSpec((rows, UNIT), lambda i: (i, 0))],
        out_specs=(
            pl.BlockSpec((rows, 256), lambda i: (i, 0)),
            pl.BlockSpec((rows // KDIM, UNIT), lambda i: (i, 0)),
        ),
        out_shape=(
            jax.ShapeDtypeStruct((tiles * KDIM, 256), BF16),
            jax.ShapeDtypeStruct((tiles, UNIT), F32),
        ),
        compiler_params=params(20, 1),
        cost_estimate=cost(tiles * KDIM * UNIT * 8, tiles * KDIM * UNIT * 8),
    )(remap_w.reshape(tiles * KDIM, UNIT))
    arrived, kept, both, inverse, incidence = lax.optimization_barrier(
        (arrived, kept, both, inverse, incidence)
    )

    land_temp, outgoing = pl.pallas_call(
        land_kernel,
        grid=(1,),
        in_specs=[
            whole(slots, 128),
            whole(REF, tiles),
            whole(tiles, 2 * REF),
            pl.BlockSpec(memory_space=pltpu.HBM),
            whole(tiles, UNIT),
            whole(tiles, UNIT),
            whole(tiles, UNIT),
            whole(tiles, UNIT),
        ],
        out_specs=(whole(tiles, UNIT), whole(slots, 128)),
        out_shape=(
            jax.ShapeDtypeStruct((tiles, UNIT), F32),
            jax.ShapeDtypeStruct((slots, 128), F32),
        ),
        scratch_shapes=[
            pltpu.VMEM((requests, 128), F32),
            pltpu.VMEM((tiles * NF, 128), F32),
            pltpu.VMEM((tiles * KDIM, 256), BF16),
            pltpu.SemaphoreType.DMA((8,)),
        ],
        compiler_params=params(50, 1),
        cost_estimate=cost(4 * requests * slots * 256 * 2, tiles * KDIM * UNIT * 4),
    )(arrived, slot_row, slot_col, both, inverse, incidence, sky_view, albedo)
    outgoing, atm_state, forcing = lax.optimization_barrier((outgoing, atm_state, forcing))
    returned = lax.all_to_all(
        outgoing.reshape(devices, CAP, 128), AXES, split_axis=0, concat_axis=0, tiled=True
    ).reshape(slots, 128)

    mixed = mix(mixing, atm_state, 0, None)
    ocean = pl.pallas_call(
        ocean_kernel,
        out_shape=jax.ShapeDtypeStruct((NF, columns), F32),
        compiler_params=params(16),
        cost_estimate=cost(columns * 100, columns * 64, columns * 4),
    )(forcing, ocean_mask.reshape(1, columns))
    returned, mixed, ocean = lax.optimization_barrier((returned, mixed, ocean))

    atm_out, col_flux = pl.pallas_call(
        finish_kernel,
        grid=(1,),
        in_specs=[
            whole(slots, 128),
            whole(devices, 128),
            whole(NF, columns),
            whole(columns, 256),
            pl.BlockSpec(memory_space=pltpu.HBM),
        ],
        out_specs=(pl.BlockSpec(memory_space=pltpu.HBM), whole(NF, columns)),
        out_shape=(
            jax.ShapeDtypeStruct((columns, NV * LEV), BF16),
            jax.ShapeDtypeStruct((NF, columns), F32),
        ),
        scratch_shapes=[
            pltpu.VMEM((columns, 256), BF16),
            pltpu.SemaphoreType.DMA((parts,)),
        ],
        input_output_aliases={4: 0},
        compiler_params=params(16, 1),
    )(returned, incoming, ocean, mixed, kept)
    return (atm_out, land_temp, col_flux)


def solution(mesh):
    return jax.shard_map(
        on_device,
        mesh=mesh,
        in_specs=(
            P(AXES, None),
            P(),
            P(),
            P(None, AXES),
            P(AXES),
            P(AXES, None),
            P(AXES, None),
            P(AXES, None, None),
            P(AXES, None),
            P(AXES, None),
            P(AXES, None),
            P(AXES, None),
            P(AXES),
            P(AXES),
        ),
        out_specs=(P(AXES, None), P(AXES, None), P(None, AXES)),
        check_vma=False,
    )
```

```python
import functools
import math

import jax
import jax.numpy as jnp
from jax import lax
from jax.experimental import pallas as pl
from jax.experimental.pallas import tpu as pltpu
from jax.sharding import PartitionSpec as P

GLL = 16
LEV = 128
NV = 4
NF = 8
SUB = 4
NEWTON = 2
NASPECT = 8
CAP = 16
UNIT = 128
REF = 4
KDIM = REF * GLL
AXES = ("sect", "lane")

F32 = jnp.float32
BF16 = jnp.bfloat16
I32 = jnp.int32
MIB = 1 << 20


def iota(shape, axis):
    return lax.broadcasted_iota(I32, shape, axis)


def matmul(left, right):
    return jnp.dot(left, right, preferred_element_type=F32)


def matmul_nt(left, right):
    return lax.dot_general(left, right, (((1,), (1,)), ((), ())), preferred_element_type=F32)


def part_of(index, size):
    return pl.ds(index * size, size)


def flag(condition):
    return jnp.where(condition, 1.0, 0.0).astype(BF16)


def high_low(values):
    high = values.astype(BF16).astype(F32)
    return high, values - high


def pair(values):
    high, low = high_low(values)
    return jnp.concatenate([high.astype(BF16), low.astype(BF16)], axis=1)


def fold(values):
    half = values.shape[1] // 2
    return values[:, :half] + values[:, half:]


def block_swap(values):
    cube = values.reshape(values.shape[0] // 8, 8, 128)
    rows, lanes = iota(cube.shape, 1), iota(cube.shape, 2)
    for step in range(3):
        reach = 1 << step
        row_bit, chunk_bit = (rows >> step) & 1, (lanes >> (4 + step)) & 1
        up = pltpu.roll(pltpu.roll(cube, 8 - reach, 1), 16 * reach, 2)
        if reach == 4:
            moved = up
        else:
            down = pltpu.roll(pltpu.roll(cube, reach, 1), 128 - 16 * reach, 2)
            moved = jnp.where(chunk_bit == 1, up, down)
        cube = jnp.where(row_bit == chunk_bit, cube, moved)
    return cube.reshape(values.shape)


def drivers(fields):
    air_temp = 1.0 + 0.05 * jnp.tanh(fields[0])
    air_humid = 0.02 / (1.0 + jnp.exp(-fields[1]))
    wind_speed = jnp.sqrt(1.0 + fields[2] * fields[2] + fields[3] * fields[3])
    return (
        air_temp,
        air_humid,
        wind_speed,
        1.5 * fields[4],
        0.5 * fields[5],
        0.6 + 0.3 * fields[6],
        fields[7],
    )


def flux_list(surface, fields, driven, absorbed, reflected, wetness):
    air_temp, air_humid, wind_speed = driven[:3]
    heat_coef = 0.1 * wind_speed
    vapor_coef = 0.25 * wind_speed * wetness
    saturation = 0.02 * jnp.exp(17.0 * (surface - 1.0))
    sensible = heat_coef * (surface - air_temp)
    latent = vapor_coef * (saturation - air_humid)
    square = surface * surface
    upward = 0.95 * (square * square)
    drag = 0.05 * wind_speed
    return [
        sensible,
        latent,
        upward,
        reflected,
        drag * fields[2],
        drag * fields[3],
        0.4 * latent,
        absorbed - upward - sensible - latent,
    ]


def start_copies(source, target, sems, parts):
    rows = target.shape[0] // parts
    copies = []
    for part in range(parts):
        span = pl.ds(part * rows, rows)
        copy = pltpu.make_async_copy(source.at[span, :], target.at[span, :], sems.at[part])
        copy.start()
        copies.append(copy)
    return copies


def route_kernel(src_ref, elem_ref, want_ref, row_ref, col_ref):
    devices, tiles = want_ref.shape[0], src_ref.shape[1]
    owner = iota((devices, tiles), 0)
    slot = iota((128, tiles), 0)
    earlier = flag(iota((tiles, tiles), 0) < iota((tiles, tiles), 1))
    base = jnp.zeros((devices, 1), F32)
    wanted = jnp.zeros((devices, 128), F32)
    places = []
    for ref in range(REF):
        source = src_ref[ref : ref + 1, :]
        hit = owner == source
        onehot = flag(hit)
        before = matmul(onehot, earlier) + base
        rank = jnp.sum(jnp.where(hit, before, 0.0), axis=0, keepdims=True)
        base = base + jnp.sum(jnp.where(hit, 1.0, 0.0), axis=1, keepdims=True)
        rank = rank.astype(I32)
        value = (elem_ref[ref : ref + 1, :] + 1).astype(F32)
        table = jnp.where(slot == rank, value, 0.0).astype(BF16)
        wanted = wanted + matmul_nt(onehot, table)
        places.append(source * CAP + rank)
    want_ref[...] = wanted.astype(I32) - 1
    for ref in range(REF):
        row_ref[ref : ref + 1, :] = places[ref]
    stacked = jnp.concatenate(places + places, axis=0).astype(F32)
    col_ref[...] = jnp.transpose(stacked).astype(I32)


def forcing_kernel(
    profile_ref,
    state_ref,
    radiation_ref,
    forcing_ref,
    blocks_ref,
    held_ref,
    sems,
):
    parts = sems.shape[0]
    copies = start_copies(state_ref, held_ref, sems, parts)
    profile = profile_ref[...]
    first = profile.astype(BF16).astype(F32)
    second = (profile - first).astype(BF16).astype(F32)
    third = profile - first - second
    rows = iota((32, LEV), 0)
    piece = jnp.where(rows < 8, first, jnp.where(rows < 16, second, jnp.where(rows < 24, third, 0.0)))
    spread = jnp.concatenate(
        [jnp.where((rows & 7) == variable, piece, 0.0) for variable in range(NV)], axis=1
    ).astype(BF16)
    size = held_ref.shape[0] // parts
    pieces = []
    for part in range(parts):
        copies[part].wait()
        columns = slice(part * size, part * size + size)
        sums = matmul_nt(spread, held_ref[columns, :])
        means = sums[0:8] + sums[8:16] + sums[16:24]
        forcing = jnp.concatenate([means[0:NV], radiation_ref[:, columns]], axis=0)
        forcing_ref[:, columns] = forcing
        pieces += [forcing[:, start : start + 128] for start in range(0, size, 128)]
    blocks_ref[...] = pair(block_swap(jnp.concatenate(pieces, axis=0)))


def reply_kernel(incoming_ref, blocks_ref, reply_ref):
    devices, elements = incoming_ref.shape[0], blocks_ref.shape[0]
    element = iota((devices, elements), 1)
    blocks = blocks_ref[...]
    incoming = incoming_ref[...]
    for slot in range(CAP):
        select = flag(element == incoming[:, slot : slot + 1])
        reply_ref[pl.ds(slot, devices, stride=CAP), :] = fold(matmul(select, blocks))


def prepare_kernel(w_ref, both_ref, inverse_ref):
    rows = w_ref.shape[0]
    part = 1024
    for start in range(0, rows, part):
        weights = w_ref[start : start + part, :]
        both_ref[start : start + part, :] = pair(weights)
        total = jnp.sum(weights.reshape(part // KDIM, KDIM, UNIT), axis=1)
        inverse_ref[start // KDIM : (start + part) // KDIM, :] = 1.0 / total


def mix_rows(mixing_ref, held_ref, size, done):
    zero = jnp.zeros((LEV, LEV), BF16)
    operator = jnp.concatenate(
        [
            jnp.concatenate([mixing_ref[0], zero], axis=1),
            jnp.concatenate([zero, mixing_ref[1]], axis=1),
        ],
        axis=0,
    )

    def work(part, carry):
        done(part, None)
        span = pl.ds(pl.multiple_of(part * size, size), size)
        state = held_ref[span, :]
        for iteration in range(SUB):
            update = matmul(state, operator)
            state = (state.astype(F32) + 0.25 * jnp.tanh(update)).astype(BF16)
        done(part, state)
        return carry

    lax.fori_loop(0, held_ref.shape[0] // size, work, 0)


def mix_kernel(half, out_half, mixing_ref, state_ref, mixed_ref, held_ref, into, out):
    parts = into.shape[0]
    size = held_ref.shape[0] // parts
    lanes = pl.ds(half * 256, 256)

    def copy_in(part):
        span = pl.ds(pl.multiple_of(part * size, size), size)
        return pltpu.make_async_copy(state_ref.at[span, lanes], held_ref.at[span, :], into.at[part])

    def copy_out(part):
        span = pl.ds(pl.multiple_of(part * size, size), size)
        return pltpu.make_async_copy(
            held_ref.at[span, :], mixed_ref.at[span, pl.ds(out_half * 256, 256)], out.at[part]
        )

    for part in range(parts):
        copy_in(part).start()

    def done(part, state):
        if state is None:
            copy_in(part).wait()
            return
        span = pl.ds(pl.multiple_of(part * size, size), size)
        if out_half is None:
            mixed_ref[span, :] = state
        else:
            held_ref[span, :] = state
            copy_out(part).start()

    mix_rows(mixing_ref, held_ref, size, done)
    if out_half is not None:
        for part in range(parts):
            copy_out(part).wait()


def ocean_kernel(forcing_ref, mask_ref, ocean_ref):
    fields = [forcing_ref[index : index + 1, :] for index in range(NF)]
    driven = drivers(fields)
    shortwave = driven[3] + driven[4]
    absorbed = 0.94 * shortwave + 0.95 * driven[5]
    one = jnp.ones_like(fields[0])
    fluxes = flux_list(one, fields, driven, absorbed, 0.06 * shortwave, one)
    mask = mask_ref[...].astype(F32)
    for index in range(NF):
        ocean_ref[index : index + 1, :] = mask * fluxes[index]


def land_kernel(
    arrived_ref,
    row_ref,
    col_ref,
    both_ref,
    inverse_ref,
    incidence_ref,
    sky_ref,
    albedo_ref,
    temp_ref,
    outgoing_ref,
    need_ref,
    raw_ref,
    held_ref,
    sems,
):
    slots = arrived_ref.shape[0]
    tiles = row_ref.shape[1]
    parts = sems.shape[0]
    copies = start_copies(both_ref, held_ref, sems, parts)
    arrived = pair(arrived_ref[...])
    slot = iota((tiles, slots), 1)
    for ref in range(REF):
        pick = flag(slot == col_ref[:, ref : ref + 1])
        need_ref[pl.ds(ref, tiles, stride=REF), :] = fold(matmul(pick, arrived))
    need_ref[...] = block_swap(need_ref[...])

    left = iota((8, 128), 1) < KDIM
    zero = jnp.zeros((8, 128), F32)

    def take(group):
        weights = held_ref[part_of(group, 256), :]
        need = need_ref[part_of(group, 16), :]
        rows = []
        for part in high_low(need):
            for half in range(2):
                block = part[half * 8 : half * 8 + 8]
                for masked in (jnp.where(left, block, 0.0), jnp.where(left, 0.0, block)):
                    rows.append(
                        jnp.concatenate([masked, zero] if half == 0 else [zero, masked], axis=1)
                    )
        product = fold(matmul(jnp.concatenate(rows, axis=0).astype(BF16), weights))
        raw_ref[part_of(group, 32), :] = product[0:32] + product[32:64]

    size = tiles // 4 // parts
    for part in range(parts):
        copies[part].wait()
        for group in range(part * size, (part + 1) * size):
            take(group)

    inverse = inverse_ref[...]
    fields = [raw_ref[pl.ds(index, tiles, stride=NF), :] * inverse for index in range(NF)]
    driven = drivers(fields)
    air_temp, air_humid, wind_speed, direct_sw, diffuse_sw, longwave, wetness = driven
    sky, albedo = sky_ref[...], albedo_ref[...]
    shortwave = direct_sw * incidence_ref[...] + diffuse_sw * sky
    absorbed = (1.0 - albedo) * shortwave + 0.95 * longwave * sky
    heat_coef = 0.1 * wind_speed
    vapor_coef = 0.25 * wind_speed * wetness
    surface = air_temp
    for iteration in range(NEWTON):
        saturation = 0.02 * jnp.exp(17.0 * (surface - 1.0))
        square = surface * surface
        imbalance = (
            absorbed
            - 0.95 * (square * square)
            - heat_coef * (surface - air_temp)
            - vapor_coef * (saturation - air_humid)
        )
        derivative = -3.8 * (square * surface) - heat_coef - 17.0 * vapor_coef * saturation
        surface = surface - imbalance / derivative
    temp_ref[...] = surface
    fluxes = flux_list(surface, fields, driven, absorbed, albedo * shortwave, wetness)
    for index in range(NF):
        raw_ref[pl.ds(index, tiles, stride=NF), :] = fluxes[index] * inverse

    def give(group):
        flux = raw_ref[part_of(group, 32), :]
        high, low = high_low(flux)
        stacked = jnp.concatenate([high, low], axis=0).astype(BF16)
        stacked = jnp.concatenate([stacked, stacked], axis=1)
        weights = held_ref[part_of(group, 256), :]
        product = matmul_nt(stacked, weights)
        product = product[0:32] + product[32:64]
        need_ref[part_of(group, 16), :] = jnp.concatenate(
            [
                jnp.where(left, product[0:8, 0:128], product[8:16, 0:128]),
                jnp.where(left, product[16:24, 128:256], product[24:32, 128:256]),
            ],
            axis=0,
        )

    for group in range(tiles // 4):
        give(group)
    need_ref[...] = block_swap(need_ref[...])
    given = jnp.concatenate(
        [pair(need_ref[pl.ds(ref, tiles, stride=REF), :]) for ref in range(REF)], axis=0
    )
    size = 512

    def place(index, carry):
        start = pl.multiple_of(index * size, size)
        spot = iota((size, tiles), 0) + start
        pick = jnp.concatenate(
            [flag(spot == row_ref[ref : ref + 1, :]) for ref in range(REF)], axis=1
        )
        outgoing_ref[pl.ds(start, size), :] = fold(matmul(pick, given))
        return carry

    lax.fori_loop(0, slots // size, place, 0, unroll=4)


def finish_kernel(
    returned_ref, incoming_ref, ocean_ref, mixed_ref, kept_ref, out_ref, flux_ref, held_ref, sems
):
    del kept_ref
    devices = incoming_ref.shape[0]
    elements = flux_ref.shape[1] // GLL
    incoming = jnp.transpose(incoming_ref[...].astype(F32)).astype(I32)
    element = iota((elements, devices), 0)
    part = jnp.zeros((elements, 256), F32)
    for slot in range(0, CAP, 2):
        select = jnp.concatenate(
            [flag(element == incoming[slot + extra : slot + extra + 1, :]) for extra in range(2)],
            axis=1,
        )
        values = jnp.concatenate(
            [pair(returned_ref[pl.ds(slot + extra, devices, stride=CAP), :]) for extra in range(2)],
            axis=0,
        )
        part = part + matmul(select, values)
    swapped = block_swap(fold(part))
    parts = sems.shape[0]
    size = held_ref.shape[0] // parts
    row, lane = iota((16, 256), 0) & 7, iota((16, 256), 1)
    first, second = (row == 0) & (lane == 0), (row == 6) & (lane == 128)
    picks = flag(first | second)
    tens, copies = [], []
    for index in range(parts):
        for start in range(index * size, index * size + size, 128):
            columns = slice(start, start + 128)
            flux = swapped[start // 16 : start // 16 + 8] + ocean_ref[:, columns]
            flux_ref[:, columns] = flux
            tens.append(0.1 * flux)
        high, low = high_low(jnp.concatenate(tens[-size // 128 :], axis=1))
        table = jnp.concatenate([high, low], axis=0).astype(BF16)
        added = lax.dot_general(
            table, picks, (((0,), (0,)), ((), ())), preferred_element_type=F32
        )
        rows = slice(index * size, index * size + size)
        held_ref[rows, :] = (mixed_ref[rows, :].astype(F32) + added).astype(BF16)
        span = pl.ds(index * size, size)
        copy = pltpu.make_async_copy(
            held_ref.at[span, :], out_ref.at[span, pl.ds(0, 256)], sems.at[index]
        )
        copy.start()
        copies.append(copy)
    for copy in copies:
        copy.wait()


def whole(*shape):
    return pl.BlockSpec(shape, lambda *_: (0,) * len(shape))


def params(mebibytes, axes=0):
    return pltpu.CompilerParams(
        vmem_limit_bytes=mebibytes * MIB,
        dimension_semantics=("arbitrary",) * axes if axes else None,
    )


def cost(flops, moved, hard=0):
    return pl.CostEstimate(flops=int(flops), bytes_accessed=int(moved), transcendentals=int(hard))


def mix(mixing, atm_state, half, out_half):
    columns = atm_state.shape[0]
    parts = 4
    apart = out_half is None
    return pl.pallas_call(
        functools.partial(mix_kernel, half, out_half),
        grid=(1,),
        in_specs=[
            pl.BlockSpec((2, LEV, LEV), lambda i: (half, 0, 0)),
            pl.BlockSpec(memory_space=pltpu.HBM),
        ],
        out_specs=whole(columns, 256) if apart else pl.BlockSpec(memory_space=pltpu.HBM),
        out_shape=jax.ShapeDtypeStruct((columns, 256 if apart else NV * LEV), BF16),
        scratch_shapes=[
            pltpu.VMEM((columns, 256), BF16),
            pltpu.SemaphoreType.DMA((parts,)),
            pltpu.SemaphoreType.DMA((parts,)),
        ],
        compiler_params=params(16, 1),
        cost_estimate=cost(columns * 256 * 256 * 2 * SUB, columns * 256 * 4, columns * 256 * SUB),
    )(mixing, atm_state)


def on_device(
    atm_state,
    profile,
    mixing,
    radiation,
    ocean_mask,
    tile_src,
    tile_elem,
    remap_w,
    slope_class,
    aspect_class,
    sky_view,
    albedo,
    sun_cos,
    sun_azimuth,
):
    devices = lax.axis_size("sect") * lax.axis_size("lane")
    columns = atm_state.shape[0]
    elements = columns // GLL
    tiles = tile_src.shape[0]
    slots = devices * CAP
    requests = tiles * REF

    wanted, slot_row, slot_col = pl.pallas_call(
        route_kernel,
        out_shape=(
            jax.ShapeDtypeStruct((devices, 128), I32),
            jax.ShapeDtypeStruct((REF, tiles), I32),
            jax.ShapeDtypeStruct((tiles, 2 * REF), I32),
        ),
        compiler_params=params(60),
    )(tile_src.T, tile_elem.T)
    wanted, atm_state = lax.optimization_barrier((wanted, atm_state))
    incoming = lax.all_to_all(wanted, AXES, split_axis=0, concat_axis=0, tiled=True)

    parts = 4
    forcing, blocks = pl.pallas_call(
        forcing_kernel,
        grid=(1,),
        in_specs=[
            whole(1, LEV),
            pl.BlockSpec(memory_space=pltpu.HBM),
            whole(4, columns),
        ],
        out_specs=(whole(NF, columns), whole(elements, 256)),
        out_shape=(
            jax.ShapeDtypeStruct((NF, columns), F32),
            jax.ShapeDtypeStruct((elements, 256), BF16),
        ),
        scratch_shapes=[
            pltpu.VMEM((columns, NV * LEV), BF16),
            pltpu.SemaphoreType.DMA((parts,)),
        ],
        compiler_params=params(50, 1),
        cost_estimate=cost(columns * 512 * 32 * 2, columns * 1024),
    )(profile.reshape(1, LEV), atm_state, radiation)
    incoming, forcing, blocks = lax.optimization_barrier((incoming, forcing, blocks))

    reply = pl.pallas_call(
        reply_kernel,
        out_shape=jax.ShapeDtypeStruct((slots, 128), F32),
        compiler_params=params(16),
        cost_estimate=cost(slots * 256 * 256 * 2, slots * 512),
    )(incoming, blocks)
    reply, atm_state, remap_w, slope_class, sun_cos = lax.optimization_barrier(
        (reply, atm_state, remap_w, slope_class, sun_cos)
    )
    arrived = lax.all_to_all(
        reply.reshape(devices, CAP, 128), AXES, split_axis=0, concat_axis=0, tiled=True
    ).reshape(slots, 128)

    kept = mix(mixing, atm_state, 1, 1)
    cosine = sun_cos[:, None]
    sine = jnp.sqrt(1.0 - cosine * cosine)
    slope_angle = slope_class.astype(F32) * 0.1
    aspect_angle = aspect_class.astype(F32) * (2.0 * math.pi / NASPECT)
    incidence = (
        jnp.maximum(
            0.0,
            jnp.cos(slope_angle) * cosine
            + jnp.sin(slope_angle) * sine * jnp.cos(sun_azimuth[:, None] - aspect_angle),
        )
        / cosine
    )
    remap_w, kept, incidence = lax.optimization_barrier((remap_w, kept, incidence))
    rows = 4096
    both, inverse = pl.pallas_call(
        prepare_kernel,
        grid=(tiles * KDIM // rows,),
        in_specs=[pl.BlockSpec((rows, UNIT), lambda i: (i, 0))],
        out_specs=(
            pl.BlockSpec((rows, 256), lambda i: (i, 0)),
            pl.BlockSpec((rows // KDIM, UNIT), lambda i: (i, 0)),
        ),
        out_shape=(
            jax.ShapeDtypeStruct((tiles * KDIM, 256), BF16),
            jax.ShapeDtypeStruct((tiles, UNIT), F32),
        ),
        compiler_params=params(20, 1),
        cost_estimate=cost(tiles * KDIM * UNIT * 8, tiles * KDIM * UNIT * 8),
    )(remap_w.reshape(tiles * KDIM, UNIT))
    arrived, kept, both, inverse, incidence = lax.optimization_barrier(
        (arrived, kept, both, inverse, incidence)
    )

    land_temp, outgoing = pl.pallas_call(
        land_kernel,
        grid=(1,),
        in_specs=[
            whole(slots, 128),
            whole(REF, tiles),
            whole(tiles, 2 * REF),
            pl.BlockSpec(memory_space=pltpu.HBM),
            whole(tiles, UNIT),
            whole(tiles, UNIT),
            whole(tiles, UNIT),
            whole(tiles, UNIT),
        ],
        out_specs=(whole(tiles, UNIT), whole(slots, 128)),
        out_shape=(
            jax.ShapeDtypeStruct((tiles, UNIT), F32),
            jax.ShapeDtypeStruct((slots, 128), F32),
        ),
        scratch_shapes=[
            pltpu.VMEM((requests, 128), F32),
            pltpu.VMEM((tiles * NF, 128), F32),
            pltpu.VMEM((tiles * KDIM, 256), BF16),
            pltpu.SemaphoreType.DMA((4,)),
        ],
        compiler_params=params(50, 1),
        cost_estimate=cost(4 * requests * slots * 256 * 2, tiles * KDIM * UNIT * 4),
    )(arrived, slot_row, slot_col, both, inverse, incidence, sky_view, albedo)
    outgoing, atm_state, forcing = lax.optimization_barrier((outgoing, atm_state, forcing))
    returned = lax.all_to_all(
        outgoing.reshape(devices, CAP, 128), AXES, split_axis=0, concat_axis=0, tiled=True
    ).reshape(slots, 128)

    mixed = mix(mixing, atm_state, 0, None)
    ocean = pl.pallas_call(
        ocean_kernel,
        out_shape=jax.ShapeDtypeStruct((NF, columns), F32),
        compiler_params=params(16),
        cost_estimate=cost(columns * 100, columns * 64, columns * 4),
    )(forcing, ocean_mask.reshape(1, columns))
    returned, mixed, ocean = lax.optimization_barrier((returned, mixed, ocean))

    atm_out, col_flux = pl.pallas_call(
        finish_kernel,
        grid=(1,),
        in_specs=[
            whole(slots, 128),
            whole(devices, 128),
            whole(NF, columns),
            whole(columns, 256),
            pl.BlockSpec(memory_space=pltpu.HBM),
        ],
        out_specs=(pl.BlockSpec(memory_space=pltpu.HBM), whole(NF, columns)),
        out_shape=(
            jax.ShapeDtypeStruct((columns, NV * LEV), BF16),
            jax.ShapeDtypeStruct((NF, columns), F32),
        ),
        scratch_shapes=[
            pltpu.VMEM((columns, 256), BF16),
            pltpu.SemaphoreType.DMA((8,)),
        ],
        input_output_aliases={4: 0},
        compiler_params=params(16, 1),
    )(returned, incoming, ocean, mixed, kept)
    return (atm_out, land_temp, col_flux)


def solution(mesh):
    return jax.shard_map(
        on_device,
        mesh=mesh,
        in_specs=(
            P(AXES, None),
            P(),
            P(),
            P(None, AXES),
            P(AXES),
            P(AXES, None),
            P(AXES, None),
            P(AXES, None, None),
            P(AXES, None),
            P(AXES, None),
            P(AXES, None),
            P(AXES, None),
            P(AXES),
            P(AXES),
        ),
        out_specs=(P(AXES, None), P(AXES, None), P(None, AXES)),
        check_vma=False,
    )
```

```python
import functools
import math

import jax
import jax.numpy as jnp
from jax import lax
from jax.experimental import pallas as pl
from jax.experimental.pallas import tpu as pltpu
from jax.sharding import PartitionSpec as P

GLL = 16
LEV = 128
NV = 4
NF = 8
SUB = 4
NEWTON = 2
NASPECT = 8
CAP = 16
UNIT = 128
REF = 4
KDIM = REF * GLL
AXES = ("sect", "lane")

F32 = jnp.float32
BF16 = jnp.bfloat16
I32 = jnp.int32
MIB = 1 << 20


def iota(shape, axis):
    return lax.broadcasted_iota(I32, shape, axis)


def matmul(left, right):
    return jnp.dot(left, right, preferred_element_type=F32)


def matmul_nt(left, right):
    return lax.dot_general(left, right, (((1,), (1,)), ((), ())), preferred_element_type=F32)


def part_of(index, size):
    return pl.ds(index * size, size)


def flag(condition):
    return jnp.where(condition, 1.0, 0.0).astype(BF16)


def high_low(values):
    high = values.astype(BF16).astype(F32)
    return high, values - high


def pair(values):
    high, low = high_low(values)
    return jnp.concatenate([high.astype(BF16), low.astype(BF16)], axis=1)


def fold(values):
    half = values.shape[1] // 2
    return values[:, :half] + values[:, half:]


def block_swap(values):
    cube = values.reshape(values.shape[0] // 8, 8, 128)
    rows, lanes = iota(cube.shape, 1), iota(cube.shape, 2)
    for step in range(3):
        reach = 1 << step
        row_bit, chunk_bit = (rows >> step) & 1, (lanes >> (4 + step)) & 1
        up = pltpu.roll(pltpu.roll(cube, 8 - reach, 1), 16 * reach, 2)
        if reach == 4:
            moved = up
        else:
            down = pltpu.roll(pltpu.roll(cube, reach, 1), 128 - 16 * reach, 2)
            moved = jnp.where(chunk_bit == 1, up, down)
        cube = jnp.where(row_bit == chunk_bit, cube, moved)
    return cube.reshape(values.shape)


def shear(values):
    return pltpu.roll(values, 0, 1, stride=16, stride_axis=0)


def turned_swap(values):
    cube = shear(values).reshape(values.shape[0] // 8, 8, 128)
    chunk = iota(cube.shape, 2) >> 4
    for reach in (1, 2, 4):
        cube = jnp.where((chunk & reach) != 0, pltpu.roll(cube, 8 - reach, 1), cube)
    return shear(cube.reshape(values.shape))


def drivers(fields):
    air_temp = 1.0 + 0.05 * jnp.tanh(fields[0])
    air_humid = 0.02 / (1.0 + jnp.exp(-fields[1]))
    wind_speed = jnp.sqrt(1.0 + fields[2] * fields[2] + fields[3] * fields[3])
    return (
        air_temp,
        air_humid,
        wind_speed,
        1.5 * fields[4],
        0.5 * fields[5],
        0.6 + 0.3 * fields[6],
        fields[7],
    )


def flux_list(surface, fields, driven, absorbed, reflected, wetness):
    air_temp, air_humid, wind_speed = driven[:3]
    heat_coef = 0.1 * wind_speed
    vapor_coef = 0.25 * wind_speed * wetness
    saturation = 0.02 * jnp.exp(17.0 * (surface - 1.0))
    sensible = heat_coef * (surface - air_temp)
    latent = vapor_coef * (saturation - air_humid)
    square = surface * surface
    upward = 0.95 * (square * square)
    drag = 0.05 * wind_speed
    return [
        sensible,
        latent,
        upward,
        reflected,
        drag * fields[2],
        drag * fields[3],
        0.4 * latent,
        absorbed - upward - sensible - latent,
    ]


def start_copies(source, target, sems, parts):
    rows = target.shape[0] // parts
    copies = []
    for part in range(parts):
        span = pl.ds(part * rows, rows)
        copy = pltpu.make_async_copy(source.at[span, :], target.at[span, :], sems.at[part])
        copy.start()
        copies.append(copy)
    return copies


def route_kernel(src_ref, elem_ref, want_ref, row_ref, col_ref):
    devices, tiles = want_ref.shape[0], src_ref.shape[1]
    owner = iota((devices, tiles), 0)
    slot = iota((128, tiles), 0)
    earlier = flag(iota((tiles, tiles), 0) < iota((tiles, tiles), 1))
    base = jnp.zeros((devices, 1), F32)
    wanted = jnp.zeros((devices, 128), F32)
    places = []
    for ref in range(REF):
        source = src_ref[ref : ref + 1, :]
        hit = owner == source
        onehot = flag(hit)
        before = matmul(onehot, earlier) + base
        rank = jnp.sum(jnp.where(hit, before, 0.0), axis=0, keepdims=True)
        base = base + jnp.sum(jnp.where(hit, 1.0, 0.0), axis=1, keepdims=True)
        rank = rank.astype(I32)
        value = (elem_ref[ref : ref + 1, :] + 1).astype(F32)
        table = jnp.where(slot == rank, value, 0.0).astype(BF16)
        wanted = wanted + matmul_nt(onehot, table)
        places.append(source * CAP + rank)
    want_ref[...] = wanted.astype(I32) - 1
    stacked = jnp.concatenate(places + places, axis=0).astype(F32)
    odd = (iota((1, tiles), 1) & 1) == 1
    turned = [
        jnp.where(odd, pltpu.roll(place, 1, 1), pltpu.roll(place, tiles - 1, 1))
        for place in places[:0:-1]
    ]
    for ref, place in enumerate([places[0]] + turned):
        row_ref[ref : ref + 1, :] = place
    col_ref[...] = jnp.transpose(stacked).astype(I32)


def forcing_kernel(
    profile_ref,
    state_ref,
    radiation_ref,
    forcing_ref,
    blocks_ref,
    held_ref,
    sems,
):
    parts = sems.shape[0]
    copies = start_copies(state_ref, held_ref, sems, parts)
    profile = profile_ref[...]
    first = profile.astype(BF16).astype(F32)
    second = (profile - first).astype(BF16).astype(F32)
    third = profile - first - second
    rows = iota((32, LEV), 0)
    piece = jnp.where(rows < 8, first, jnp.where(rows < 16, second, jnp.where(rows < 24, third, 0.0)))
    spread = jnp.concatenate(
        [jnp.where((rows & 7) == variable, piece, 0.0) for variable in range(NV)], axis=1
    ).astype(BF16)
    size = held_ref.shape[0] // parts
    pieces = []
    for part in range(parts):
        copies[part].wait()
        columns = slice(part * size, part * size + size)
        sums = matmul_nt(spread, held_ref[columns, :])
        means = sums[0:8] + sums[8:16] + sums[16:24]
        forcing = jnp.concatenate([means[0:NV], radiation_ref[:, columns]], axis=0)
        forcing_ref[:, columns] = forcing
        pieces += [forcing[:, start : start + 128] for start in range(0, size, 128)]
    blocks_ref[...] = pair(block_swap(jnp.concatenate(pieces, axis=0)))


def send_part(held, target, sems, part, size):
    span = pl.ds(part * size, size)
    copy = pltpu.make_async_copy(held.at[span, :], target.at[span, :], sems.at[part])
    copy.start()
    return copy


def reply_kernel(incoming_ref, blocks_ref, reply_ref, held_ref, sems):
    parts = sems.shape[0]
    devices, elements = incoming_ref.shape[0] // parts, blocks_ref.shape[0]
    element = iota((devices, elements), 1)
    blocks = blocks_ref[...]
    copies = []
    for part in range(parts):
        incoming = incoming_ref[part * devices : (part + 1) * devices, :]
        select = jnp.concatenate(
            [flag(element == incoming[:, slot : slot + 1]) for slot in range(CAP)], axis=0
        )
        values = fold(matmul(select, blocks))
        for slot in range(CAP):
            held_ref[pl.ds(part * devices * CAP + slot, devices, stride=CAP), :] = values[
                slot * devices : (slot + 1) * devices
            ]
        copies.append(send_part(held_ref, reply_ref, sems, part, devices * CAP))
    for copy in copies:
        copy.wait()


def prepare_kernel(w_ref, both_ref, inverse_ref):
    rows = w_ref.shape[0]
    part = 1024
    for start in range(0, rows, part):
        weights = w_ref[start : start + part, :]
        both_ref[start : start + part, :] = pair(weights)
        total = jnp.sum(weights.reshape(part // KDIM, KDIM, UNIT), axis=1)
        inverse_ref[start // KDIM : (start + part) // KDIM, :] = 1.0 / total


def mix_rows(mixing_ref, held_ref, size, done):
    zero = jnp.zeros((LEV, LEV), BF16)
    operator = jnp.concatenate(
        [
            jnp.concatenate([mixing_ref[0], zero], axis=1),
            jnp.concatenate([zero, mixing_ref[1]], axis=1),
        ],
        axis=0,
    )

    def work(part, carry):
        done(part, None)
        span = pl.ds(pl.multiple_of(part * size, size), size)
        state = held_ref[span, :]
        for iteration in range(SUB):
            update = matmul(state, operator)
            state = (state.astype(F32) + 0.25 * jnp.tanh(update)).astype(BF16)
        done(part, state)
        return carry

    lax.fori_loop(0, held_ref.shape[0] // size, work, 0)


def mix_kernel(half, out_half, mixing_ref, state_ref, mixed_ref, held_ref, into, out):
    parts = into.shape[0]
    size = held_ref.shape[0] // parts
    lanes = pl.ds(half * 256, 256)

    def copy_in(part):
        span = pl.ds(pl.multiple_of(part * size, size), size)
        return pltpu.make_async_copy(state_ref.at[span, lanes], held_ref.at[span, :], into.at[part])

    def copy_out(part):
        span = pl.ds(pl.multiple_of(part * size, size), size)
        return pltpu.make_async_copy(
            held_ref.at[span, :], mixed_ref.at[span, pl.ds(out_half * 256, 256)], out.at[part]
        )

    for part in range(parts):
        copy_in(part).start()

    def done(part, state):
        if state is None:
            copy_in(part).wait()
            return
        span = pl.ds(pl.multiple_of(part * size, size), size)
        if out_half is None:
            mixed_ref[span, :] = state
        else:
            held_ref[span, :] = state
            copy_out(part).start()

    mix_rows(mixing_ref, held_ref, size, done)
    if out_half is not None:
        for part in range(parts):
            copy_out(part).wait()


def ocean_kernel(forcing_ref, mask_ref, ocean_ref):
    fields = [forcing_ref[index : index + 1, :] for index in range(NF)]
    driven = drivers(fields)
    shortwave = driven[3] + driven[4]
    absorbed = 0.94 * shortwave + 0.95 * driven[5]
    one = jnp.ones_like(fields[0])
    fluxes = flux_list(one, fields, driven, absorbed, 0.06 * shortwave, one)
    mask = mask_ref[...].astype(F32)
    for index in range(NF):
        ocean_ref[index : index + 1, :] = mask * fluxes[index]


def land_kernel(
    arrived_ref,
    row_ref,
    col_ref,
    both_ref,
    inverse_ref,
    incidence_ref,
    sky_ref,
    albedo_ref,
    temp_ref,
    outgoing_ref,
    need_ref,
    raw_ref,
    held_ref,
    sems,
):
    slots = arrived_ref.shape[0]
    tiles = row_ref.shape[1]
    parts = sems.shape[0]
    copies = start_copies(both_ref, held_ref, sems, parts)
    arrived = pair(arrived_ref[...])
    slot = iota((tiles, slots), 1)
    for ref in range(REF):
        pick = flag(slot == col_ref[:, ref : ref + 1])
        need_ref[pl.ds(ref, tiles, stride=REF), :] = fold(matmul(pick, arrived))
    need_ref[...] = turned_swap(need_ref[...])

    left = iota((8, 128), 1) < KDIM
    zero = jnp.zeros((8, 128), F32)

    def take(group):
        weights = held_ref[part_of(group, 256), :]
        need = need_ref[part_of(group, 16), :]
        rows = []
        for part in high_low(need):
            for half in range(2):
                block = part[half * 8 : half * 8 + 8]
                for masked in (jnp.where(left, block, 0.0), jnp.where(left, 0.0, block)):
                    rows.append(
                        jnp.concatenate([masked, zero] if half == 0 else [zero, masked], axis=1)
                    )
        product = fold(matmul(jnp.concatenate(rows, axis=0).astype(BF16), weights))
        raw_ref[part_of(group, 32), :] = product[0:32] + product[32:64]

    size = tiles // 4 // parts
    for part in range(parts):
        copies[part].wait()
        for group in range(part * size, (part + 1) * size):
            take(group)

    inverse = inverse_ref[...]
    fields = [
        raw_ref[pl.ds((NF - index) % NF, tiles, stride=NF), :] * inverse for index in range(NF)
    ]
    driven = drivers(fields)
    air_temp, air_humid, wind_speed, direct_sw, diffuse_sw, longwave, wetness = driven
    sky, albedo = sky_ref[...], albedo_ref[...]
    shortwave = direct_sw * incidence_ref[...] + diffuse_sw * sky
    absorbed = (1.0 - albedo) * shortwave + 0.95 * longwave * sky
    heat_coef = 0.1 * wind_speed
    vapor_coef = 0.25 * wind_speed * wetness
    surface = air_temp
    for iteration in range(NEWTON):
        saturation = 0.02 * jnp.exp(17.0 * (surface - 1.0))
        square = surface * surface
        imbalance = (
            absorbed
            - 0.95 * (square * square)
            - heat_coef * (surface - air_temp)
            - vapor_coef * (saturation - air_humid)
        )
        derivative = -3.8 * (square * surface) - heat_coef - 17.0 * vapor_coef * saturation
        surface = surface - imbalance / derivative
    temp_ref[...] = surface
    fluxes = flux_list(surface, fields, driven, absorbed, albedo * shortwave, wetness)
    for index in range(NF):
        raw_ref[pl.ds((NF - index) % NF, tiles, stride=NF), :] = fluxes[index] * inverse

    def give(group):
        flux = raw_ref[part_of(group, 32), :]
        high, low = high_low(flux)
        stacked = jnp.concatenate([high, low], axis=0).astype(BF16)
        stacked = jnp.concatenate([stacked, stacked], axis=1)
        weights = held_ref[part_of(group, 256), :]
        product = matmul_nt(stacked, weights)
        product = product[0:32] + product[32:64]
        need_ref[part_of(group, 16), :] = jnp.concatenate(
            [
                jnp.where(left, product[0:8, 0:128], product[8:16, 0:128]),
                jnp.where(left, product[16:24, 128:256], product[24:32, 128:256]),
            ],
            axis=0,
        )

    for group in range(tiles // 4):
        give(group)
    need_ref[...] = turned_swap(need_ref[...])
    given = jnp.concatenate(
        [pair(need_ref[pl.ds(ref, tiles, stride=REF), :]) for ref in range(REF)], axis=0
    )
    size = 512

    def place(index, carry):
        start = pl.multiple_of(index * size, size)
        spot = iota((size, tiles), 0) + start
        pick = jnp.concatenate(
            [flag(spot == row_ref[ref : ref + 1, :]) for ref in range(REF)], axis=1
        )
        outgoing_ref[pl.ds(start, size), :] = fold(matmul(pick, given))
        return carry

    lax.fori_loop(0, slots // size, place, 0, unroll=4)


def finish_kernel(
    returned_ref, incoming_ref, ocean_ref, mixed_ref, kept_ref, out_ref, flux_ref, held_ref, sems
):
    del kept_ref
    devices = incoming_ref.shape[0]
    elements = flux_ref.shape[1] // GLL
    incoming = jnp.transpose(incoming_ref[...].astype(F32)).astype(I32)
    element = iota((elements, devices), 0)
    part = jnp.zeros((elements, 256), F32)
    for slot in range(0, CAP, 2):
        select = jnp.concatenate(
            [flag(element == incoming[slot + extra : slot + extra + 1, :]) for extra in range(2)],
            axis=1,
        )
        values = jnp.concatenate(
            [pair(returned_ref[pl.ds(slot + extra, devices, stride=CAP), :]) for extra in range(2)],
            axis=0,
        )
        part = part + matmul(select, values)
    swapped = turned_swap(fold(part))
    parts = sems.shape[0]
    size = held_ref.shape[0] // parts
    row, lane = iota((16, 256), 0) & 7, iota((16, 256), 1)
    first, second = (row == 0) & (lane == 0), (row == 6) & (lane == 128)
    picks = flag(first | second)
    tens, copies = [], []
    for index in range(parts):
        for start in range(index * size, index * size + size, 128):
            columns = slice(start, start + 128)
            flux = swapped[start // 16 : start // 16 + 8] + ocean_ref[:, columns]
            flux_ref[:, columns] = flux
            tens.append(0.1 * flux)
        high, low = high_low(jnp.concatenate(tens[-size // 128 :], axis=1))
        table = jnp.concatenate([high, low], axis=0).astype(BF16)
        added = lax.dot_general(
            table, picks, (((0,), (0,)), ((), ())), preferred_element_type=F32
        )
        rows = slice(index * size, index * size + size)
        held_ref[rows, :] = (mixed_ref[rows, :].astype(F32) + added).astype(BF16)
        span = pl.ds(index * size, size)
        copy = pltpu.make_async_copy(
            held_ref.at[span, :], out_ref.at[span, pl.ds(0, 256)], sems.at[index]
        )
        copy.start()
        copies.append(copy)
    for copy in copies:
        copy.wait()


def whole(*shape):
    return pl.BlockSpec(shape, lambda *_: (0,) * len(shape))


def params(mebibytes, axes=0):
    return pltpu.CompilerParams(
        vmem_limit_bytes=mebibytes * MIB,
        dimension_semantics=("arbitrary",) * axes if axes else None,
    )


def cost(flops, moved, hard=0):
    return pl.CostEstimate(flops=int(flops), bytes_accessed=int(moved), transcendentals=int(hard))


def mix(mixing, atm_state, half, out_half):
    columns = atm_state.shape[0]
    parts = 4
    apart = out_half is None
    return pl.pallas_call(
        functools.partial(mix_kernel, half, out_half),
        grid=(1,),
        in_specs=[
            pl.BlockSpec((2, LEV, LEV), lambda i: (half, 0, 0)),
            pl.BlockSpec(memory_space=pltpu.HBM),
        ],
        out_specs=whole(columns, 256) if apart else pl.BlockSpec(memory_space=pltpu.HBM),
        out_shape=jax.ShapeDtypeStruct((columns, 256 if apart else NV * LEV), BF16),
        scratch_shapes=[
            pltpu.VMEM((columns, 256), BF16),
            pltpu.SemaphoreType.DMA((parts,)),
            pltpu.SemaphoreType.DMA((parts,)),
        ],
        compiler_params=params(16, 1),
        cost_estimate=cost(columns * 256 * 256 * 2 * SUB, columns * 256 * 4, columns * 256 * SUB),
    )(mixing, atm_state)


def on_device(
    atm_state,
    profile,
    mixing,
    radiation,
    ocean_mask,
    tile_src,
    tile_elem,
    remap_w,
    slope_class,
    aspect_class,
    sky_view,
    albedo,
    sun_cos,
    sun_azimuth,
):
    devices = lax.axis_size("sect") * lax.axis_size("lane")
    columns = atm_state.shape[0]
    elements = columns // GLL
    tiles = tile_src.shape[0]
    slots = devices * CAP
    requests = tiles * REF

    wanted, slot_row, slot_col = pl.pallas_call(
        route_kernel,
        out_shape=(
            jax.ShapeDtypeStruct((devices, 128), I32),
            jax.ShapeDtypeStruct((REF, tiles), I32),
            jax.ShapeDtypeStruct((tiles, 2 * REF), I32),
        ),
        compiler_params=params(60),
    )(tile_src.T, tile_elem.T)
    wanted, atm_state = lax.optimization_barrier((wanted, atm_state))
    incoming = lax.all_to_all(wanted, AXES, split_axis=0, concat_axis=0, tiled=True)

    parts = 4
    forcing, blocks = pl.pallas_call(
        forcing_kernel,
        grid=(1,),
        in_specs=[
            whole(1, LEV),
            pl.BlockSpec(memory_space=pltpu.HBM),
            whole(4, columns),
        ],
        out_specs=(whole(NF, columns), whole(elements, 256)),
        out_shape=(
            jax.ShapeDtypeStruct((NF, columns), F32),
            jax.ShapeDtypeStruct((elements, 256), BF16),
        ),
        scratch_shapes=[
            pltpu.VMEM((columns, NV * LEV), BF16),
            pltpu.SemaphoreType.DMA((parts,)),
        ],
        compiler_params=params(50, 1),
        cost_estimate=cost(columns * 512 * 32 * 2, columns * 1024),
    )(profile.reshape(1, LEV), atm_state, radiation)
    incoming, forcing, blocks = lax.optimization_barrier((incoming, forcing, blocks))

    reply = pl.pallas_call(
        reply_kernel,
        grid=(1,),
        in_specs=[whole(devices, 128), whole(elements, 256)],
        out_specs=pl.BlockSpec(memory_space=pltpu.HBM),
        out_shape=jax.ShapeDtypeStruct((slots, 128), F32),
        scratch_shapes=[pltpu.VMEM((slots, 128), F32), pltpu.SemaphoreType.DMA((4,))],
        compiler_params=params(16, 1),
        cost_estimate=cost(slots * 256 * 256 * 2, slots * 512),
    )(incoming, blocks)
    reply, remap_w, slope_class, sun_cos = lax.optimization_barrier(
        (reply, remap_w, slope_class, sun_cos)
    )
    arrived = lax.all_to_all(
        reply.reshape(devices, CAP, 128), AXES, split_axis=0, concat_axis=0, tiled=True
    ).reshape(slots, 128)

    cosine = sun_cos[:, None]
    sine = jnp.sqrt(1.0 - cosine * cosine)
    slope_angle = slope_class.astype(F32) * 0.1
    aspect_angle = aspect_class.astype(F32) * (2.0 * math.pi / NASPECT)
    incidence = (
        jnp.maximum(
            0.0,
            jnp.cos(slope_angle) * cosine
            + jnp.sin(slope_angle) * sine * jnp.cos(sun_azimuth[:, None] - aspect_angle),
        )
        / cosine
    )
    rows = 4096
    both, inverse = pl.pallas_call(
        prepare_kernel,
        grid=(tiles * KDIM // rows,),
        in_specs=[pl.BlockSpec((rows, UNIT), lambda i: (i, 0))],
        out_specs=(
            pl.BlockSpec((rows, 256), lambda i: (i, 0)),
            pl.BlockSpec((rows // KDIM, UNIT), lambda i: (i, 0)),
        ),
        out_shape=(
            jax.ShapeDtypeStruct((tiles * KDIM, 256), BF16),
            jax.ShapeDtypeStruct((tiles, UNIT), F32),
        ),
        compiler_params=params(20, 1),
        cost_estimate=cost(tiles * KDIM * UNIT * 8, tiles * KDIM * UNIT * 8),
    )(remap_w.reshape(tiles * KDIM, UNIT))
    arrived, both, inverse, incidence = lax.optimization_barrier(
        (arrived, both, inverse, incidence)
    )

    land_temp, outgoing = pl.pallas_call(
        land_kernel,
        grid=(1,),
        in_specs=[
            whole(slots, 128),
            whole(REF, tiles),
            whole(tiles, 2 * REF),
            pl.BlockSpec(memory_space=pltpu.HBM),
            whole(tiles, UNIT),
            whole(tiles, UNIT),
            whole(tiles, UNIT),
            whole(tiles, UNIT),
        ],
        out_specs=(whole(tiles, UNIT), whole(slots, 128)),
        out_shape=(
            jax.ShapeDtypeStruct((tiles, UNIT), F32),
            jax.ShapeDtypeStruct((slots, 128), F32),
        ),
        scratch_shapes=[
            pltpu.VMEM((requests, 128), F32),
            pltpu.VMEM((tiles * NF, 128), F32),
            pltpu.VMEM((tiles * KDIM, 256), BF16),
            pltpu.SemaphoreType.DMA((4,)),
        ],
        compiler_params=params(50, 1),
        cost_estimate=cost(4 * requests * slots * 256 * 2, tiles * KDIM * UNIT * 4),
    )(arrived, slot_row, slot_col, both, inverse, incidence, sky_view, albedo)
    outgoing, atm_state, forcing = lax.optimization_barrier((outgoing, atm_state, forcing))
    returned = lax.all_to_all(
        outgoing.reshape(devices, CAP, 128), AXES, split_axis=0, concat_axis=0, tiled=True
    ).reshape(slots, 128)

    mixed = mix(mixing, atm_state, 0, None)
    kept = mix(mixing, atm_state, 1, 1)
    ocean = pl.pallas_call(
        ocean_kernel,
        out_shape=jax.ShapeDtypeStruct((NF, columns), F32),
        compiler_params=params(16),
        cost_estimate=cost(columns * 100, columns * 64, columns * 4),
    )(forcing, ocean_mask.reshape(1, columns))
    returned, mixed, kept, ocean = lax.optimization_barrier((returned, mixed, kept, ocean))

    atm_out, col_flux = pl.pallas_call(
        finish_kernel,
        grid=(1,),
        in_specs=[
            whole(slots, 128),
            whole(devices, 128),
            whole(NF, columns),
            whole(columns, 256),
            pl.BlockSpec(memory_space=pltpu.HBM),
        ],
        out_specs=(pl.BlockSpec(memory_space=pltpu.HBM), whole(NF, columns)),
        out_shape=(
            jax.ShapeDtypeStruct((columns, NV * LEV), BF16),
            jax.ShapeDtypeStruct((NF, columns), F32),
        ),
        scratch_shapes=[
            pltpu.VMEM((columns, 256), BF16),
            pltpu.SemaphoreType.DMA((8,)),
        ],
        input_output_aliases={4: 0},
        compiler_params=params(16, 1),
    )(returned, incoming, ocean, mixed, kept)
    return (atm_out, land_temp, col_flux)


def solution(mesh):
    return jax.shard_map(
        on_device,
        mesh=mesh,
        in_specs=(
            P(AXES, None),
            P(),
            P(),
            P(None, AXES),
            P(AXES),
            P(AXES, None),
            P(AXES, None),
            P(AXES, None, None),
            P(AXES, None),
            P(AXES, None),
            P(AXES, None),
            P(AXES, None),
            P(AXES),
            P(AXES),
        ),
        out_specs=(P(AXES, None), P(AXES, None), P(None, AXES)),
        check_vma=False,
    )
```

```python
import functools
import math

import jax
import jax.numpy as jnp
from jax import lax
from jax.experimental import pallas as pl
from jax.experimental.pallas import tpu as pltpu
from jax.sharding import PartitionSpec as P

GLL = 16
LEV = 128
NV = 4
NF = 8
SUB = 4
NEWTON = 2
NASPECT = 8
CAP = 16
UNIT = 128
REF = 4
KDIM = REF * GLL
AXES = ("sect", "lane")

F32 = jnp.float32
BF16 = jnp.bfloat16
I32 = jnp.int32
MIB = 1 << 20


def iota(shape, axis):
    return lax.broadcasted_iota(I32, shape, axis)


def matmul(left, right):
    return jnp.dot(left, right, preferred_element_type=F32)


def matmul_nt(left, right):
    return lax.dot_general(left, right, (((1,), (1,)), ((), ())), preferred_element_type=F32)


def part_of(index, size):
    return pl.ds(index * size, size)


def flag(condition):
    return jnp.where(condition, 1.0, 0.0).astype(BF16)


def high_low(values):
    high = values.astype(BF16).astype(F32)
    return high, values - high


def pair(values):
    high, low = high_low(values)
    return jnp.concatenate([high.astype(BF16), low.astype(BF16)], axis=1)


def fold(values):
    half = values.shape[1] // 2
    return values[:, :half] + values[:, half:]


def block_swap(values):
    cube = values.reshape(values.shape[0] // 8, 8, 128)
    rows, lanes = iota(cube.shape, 1), iota(cube.shape, 2)
    for step in range(3):
        reach = 1 << step
        row_bit, chunk_bit = (rows >> step) & 1, (lanes >> (4 + step)) & 1
        up = pltpu.roll(pltpu.roll(cube, 8 - reach, 1), 16 * reach, 2)
        if reach == 4:
            moved = up
        else:
            down = pltpu.roll(pltpu.roll(cube, reach, 1), 128 - 16 * reach, 2)
            moved = jnp.where(chunk_bit == 1, up, down)
        cube = jnp.where(row_bit == chunk_bit, cube, moved)
    return cube.reshape(values.shape)


def shear(values):
    return pltpu.roll(values, 0, 1, stride=16, stride_axis=0)


def turned_swap(values):
    cube = shear(values).reshape(values.shape[0] // 8, 8, 128)
    chunk = iota(cube.shape, 2) >> 4
    for reach in (1, 2, 4):
        cube = jnp.where((chunk & reach) != 0, pltpu.roll(cube, 8 - reach, 1), cube)
    return shear(cube.reshape(values.shape))


def drivers(fields):
    air_temp = 1.0 + 0.05 * jnp.tanh(fields[0])
    air_humid = 0.02 / (1.0 + jnp.exp(-fields[1]))
    wind_speed = jnp.sqrt(1.0 + fields[2] * fields[2] + fields[3] * fields[3])
    return (
        air_temp,
        air_humid,
        wind_speed,
        1.5 * fields[4],
        0.5 * fields[5],
        0.6 + 0.3 * fields[6],
        fields[7],
    )


def flux_list(surface, fields, driven, absorbed, reflected, wetness):
    air_temp, air_humid, wind_speed = driven[:3]
    heat_coef = 0.1 * wind_speed
    vapor_coef = 0.25 * wind_speed * wetness
    saturation = 0.02 * jnp.exp(17.0 * (surface - 1.0))
    sensible = heat_coef * (surface - air_temp)
    latent = vapor_coef * (saturation - air_humid)
    square = surface * surface
    upward = 0.95 * (square * square)
    drag = 0.05 * wind_speed
    return [
        sensible,
        latent,
        upward,
        reflected,
        drag * fields[2],
        drag * fields[3],
        0.4 * latent,
        absorbed - upward - sensible - latent,
    ]


def start_copies(source, target, sems, parts):
    rows = target.shape[0] // parts
    copies = []
    for part in range(parts):
        span = pl.ds(part * rows, rows)
        copy = pltpu.make_async_copy(source.at[span, :], target.at[span, :], sems.at[part])
        copy.start()
        copies.append(copy)
    return copies


def route_kernel(src_ref, elem_ref, want_ref, row_ref, col_ref):
    devices, tiles = want_ref.shape[0], src_ref.shape[1]
    owner = iota((devices, tiles), 0)
    slot = iota((128, tiles), 0)
    earlier = flag(iota((tiles, tiles), 0) < iota((tiles, tiles), 1))
    base = jnp.zeros((devices, 1), F32)
    wanted = jnp.zeros((devices, 128), F32)
    places = []
    for ref in range(REF):
        source = src_ref[ref : ref + 1, :]
        hit = owner == source
        onehot = flag(hit)
        before = matmul(onehot, earlier) + base
        rank = jnp.sum(jnp.where(hit, before, 0.0), axis=0, keepdims=True)
        base = base + jnp.sum(jnp.where(hit, 1.0, 0.0), axis=1, keepdims=True)
        rank = rank.astype(I32)
        value = (elem_ref[ref : ref + 1, :] + 1).astype(F32)
        table = jnp.where(slot == rank, value, 0.0).astype(BF16)
        wanted = wanted + matmul_nt(onehot, table)
        places.append(source * CAP + rank)
    want_ref[...] = wanted.astype(I32) - 1
    stacked = jnp.concatenate(places + places, axis=0).astype(F32)
    odd = (iota((1, tiles), 1) & 1) == 1
    turned = [
        jnp.where(odd, pltpu.roll(place, 1, 1), pltpu.roll(place, tiles - 1, 1))
        for place in places[:0:-1]
    ]
    for ref, place in enumerate([places[0]] + turned):
        row_ref[ref : ref + 1, :] = place
    col_ref[...] = jnp.transpose(stacked).astype(I32)


def forcing_kernel(
    profile_ref,
    state_ref,
    radiation_ref,
    forcing_ref,
    blocks_ref,
    held_ref,
    sems,
):
    parts = sems.shape[0]
    copies = start_copies(state_ref, held_ref, sems, parts)
    profile = profile_ref[...]
    first = profile.astype(BF16).astype(F32)
    second = (profile - first).astype(BF16).astype(F32)
    third = profile - first - second
    rows = iota((32, LEV), 0)
    piece = jnp.where(rows < 8, first, jnp.where(rows < 16, second, jnp.where(rows < 24, third, 0.0)))
    spread = jnp.concatenate(
        [jnp.where((rows & 7) == variable, piece, 0.0) for variable in range(NV)], axis=1
    ).astype(BF16)
    size = held_ref.shape[0] // parts
    pieces = []
    for part in range(parts):
        copies[part].wait()
        columns = slice(part * size, part * size + size)
        sums = matmul_nt(spread, held_ref[columns, :])
        means = sums[0:8] + sums[8:16] + sums[16:24]
        forcing = jnp.concatenate([means[0:NV], radiation_ref[:, columns]], axis=0)
        forcing_ref[:, columns] = forcing
        pieces += [forcing[:, start : start + 128] for start in range(0, size, 128)]
    blocks_ref[...] = pair(block_swap(jnp.concatenate(pieces, axis=0)))


def send_part(held, target, sems, part, size):
    span = pl.ds(part * size, size)
    copy = pltpu.make_async_copy(held.at[span, :], target.at[span, :], sems.at[part])
    copy.start()
    return copy


def reply_kernel(incoming_ref, blocks_ref, reply_ref, held_ref, sems):
    parts = sems.shape[0]
    devices, elements = incoming_ref.shape[0] // parts, blocks_ref.shape[0]
    element = iota((devices, elements), 1)
    blocks = blocks_ref[...]
    copies = []
    for part in range(parts):
        incoming = incoming_ref[part * devices : (part + 1) * devices, :]
        select = jnp.concatenate(
            [flag(element == incoming[:, slot : slot + 1]) for slot in range(CAP)], axis=0
        )
        values = fold(matmul(select, blocks))
        for slot in range(CAP):
            held_ref[pl.ds(part * devices * CAP + slot, devices, stride=CAP), :] = values[
                slot * devices : (slot + 1) * devices
            ]
        copies.append(send_part(held_ref, reply_ref, sems, part, devices * CAP))
    for copy in copies:
        copy.wait()


def prepare_kernel(w_ref, both_ref, inverse_ref):
    rows = w_ref.shape[0]
    part = 1024
    for start in range(0, rows, part):
        weights = w_ref[start : start + part, :]
        both_ref[start : start + part, :] = pair(weights)
        total = jnp.sum(weights.reshape(part // KDIM, KDIM, UNIT), axis=1)
        inverse_ref[start // KDIM : (start + part) // KDIM, :] = 1.0 / total


def mix_rows(mixing_ref, held_ref, size, done):
    zero = jnp.zeros((LEV, LEV), BF16)
    operator = jnp.concatenate(
        [
            jnp.concatenate([mixing_ref[0], zero], axis=1),
            jnp.concatenate([zero, mixing_ref[1]], axis=1),
        ],
        axis=0,
    )

    def work(part, carry):
        done(part, None)
        span = pl.ds(pl.multiple_of(part * size, size), size)
        state = held_ref[span, :]
        for iteration in range(SUB):
            update = matmul(state, operator)
            state = (state.astype(F32) + 0.25 * jnp.tanh(update)).astype(BF16)
        done(part, state)
        return carry

    lax.fori_loop(0, held_ref.shape[0] // size, work, 0)


def mix_kernel(half, out_half, mixing_ref, state_ref, mixed_ref, held_ref, into, out):
    parts = into.shape[0]
    size = held_ref.shape[0] // parts
    lanes = pl.ds(half * 256, 256)

    def copy_in(part):
        span = pl.ds(pl.multiple_of(part * size, size), size)
        return pltpu.make_async_copy(state_ref.at[span, lanes], held_ref.at[span, :], into.at[part])

    def copy_out(part):
        span = pl.ds(pl.multiple_of(part * size, size), size)
        return pltpu.make_async_copy(
            held_ref.at[span, :], mixed_ref.at[span, pl.ds(out_half * 256, 256)], out.at[part]
        )

    for part in range(parts):
        copy_in(part).start()

    def done(part, state):
        if state is None:
            copy_in(part).wait()
            return
        span = pl.ds(pl.multiple_of(part * size, size), size)
        if out_half is None:
            mixed_ref[span, :] = state
        else:
            held_ref[span, :] = state
            copy_out(part).start()

    mix_rows(mixing_ref, held_ref, size, done)
    if out_half is not None:
        for part in range(parts):
            copy_out(part).wait()


def ocean_kernel(forcing_ref, mask_ref, ocean_ref):
    fields = [forcing_ref[index : index + 1, :] for index in range(NF)]
    driven = drivers(fields)
    shortwave = driven[3] + driven[4]
    absorbed = 0.94 * shortwave + 0.95 * driven[5]
    one = jnp.ones_like(fields[0])
    fluxes = flux_list(one, fields, driven, absorbed, 0.06 * shortwave, one)
    mask = mask_ref[...].astype(F32)
    for index in range(NF):
        ocean_ref[index : index + 1, :] = mask * fluxes[index]


def land_kernel(
    arrived_ref,
    row_ref,
    col_ref,
    both_ref,
    inverse_ref,
    incidence_ref,
    sky_ref,
    albedo_ref,
    temp_ref,
    outgoing_ref,
    need_ref,
    raw_ref,
    held_ref,
    sems,
):
    slots = arrived_ref.shape[0]
    tiles = row_ref.shape[1]
    parts = sems.shape[0]
    copies = start_copies(both_ref, held_ref, sems, parts)
    arrived = pair(arrived_ref[...])
    slot = iota((tiles, slots), 1)
    for ref in range(REF):
        pick = flag(slot == col_ref[:, ref : ref + 1])
        need_ref[pl.ds(ref, tiles, stride=REF), :] = fold(matmul(pick, arrived))
    need_ref[...] = turned_swap(need_ref[...])

    left = iota((8, 128), 1) < KDIM
    zero = jnp.zeros((8, 128), F32)

    def take(group):
        weights = held_ref[part_of(group, 256), :]
        need = need_ref[part_of(group, 16), :]
        rows = []
        for part in high_low(need):
            for half in range(2):
                block = part[half * 8 : half * 8 + 8]
                for masked in (jnp.where(left, block, 0.0), jnp.where(left, 0.0, block)):
                    rows.append(
                        jnp.concatenate([masked, zero] if half == 0 else [zero, masked], axis=1)
                    )
        product = fold(matmul(jnp.concatenate(rows, axis=0).astype(BF16), weights))
        raw_ref[part_of(group, 32), :] = product[0:32] + product[32:64]

    size = tiles // 4 // parts
    for part in range(parts):
        copies[part].wait()
        for group in range(part * size, (part + 1) * size):
            take(group)

    inverse = inverse_ref[...]
    fields = [
        raw_ref[pl.ds((NF - index) % NF, tiles, stride=NF), :] * inverse for index in range(NF)
    ]
    driven = drivers(fields)
    air_temp, air_humid, wind_speed, direct_sw, diffuse_sw, longwave, wetness = driven
    sky, albedo = sky_ref[...], albedo_ref[...]
    shortwave = direct_sw * incidence_ref[...] + diffuse_sw * sky
    absorbed = (1.0 - albedo) * shortwave + 0.95 * longwave * sky
    heat_coef = 0.1 * wind_speed
    vapor_coef = 0.25 * wind_speed * wetness
    surface = air_temp
    for iteration in range(NEWTON):
        saturation = 0.02 * jnp.exp(17.0 * (surface - 1.0))
        square = surface * surface
        imbalance = (
            absorbed
            - 0.95 * (square * square)
            - heat_coef * (surface - air_temp)
            - vapor_coef * (saturation - air_humid)
        )
        derivative = -3.8 * (square * surface) - heat_coef - 17.0 * vapor_coef * saturation
        surface = surface - imbalance / derivative
    temp_ref[...] = surface
    fluxes = flux_list(surface, fields, driven, absorbed, albedo * shortwave, wetness)
    for index in range(NF):
        raw_ref[pl.ds((NF - index) % NF, tiles, stride=NF), :] = fluxes[index] * inverse

    def give(group):
        flux = raw_ref[part_of(group, 32), :]
        high, low = high_low(flux)
        stacked = jnp.concatenate([high, low], axis=0).astype(BF16)
        stacked = jnp.concatenate([stacked, stacked], axis=1)
        weights = held_ref[part_of(group, 256), :]
        product = matmul_nt(stacked, weights)
        product = product[0:32] + product[32:64]
        need_ref[part_of(group, 16), :] = jnp.concatenate(
            [
                jnp.where(left, product[0:8, 0:128], product[8:16, 0:128]),
                jnp.where(left, product[16:24, 128:256], product[24:32, 128:256]),
            ],
            axis=0,
        )

    for group in range(tiles // 4):
        give(group)
    need_ref[...] = turned_swap(need_ref[...])
    given = jnp.concatenate(
        [pair(need_ref[pl.ds(ref, tiles, stride=REF), :]) for ref in range(REF)], axis=0
    )
    size = 512

    def place(index, carry):
        start = pl.multiple_of(index * size, size)
        spot = iota((size, tiles), 0) + start
        pick = jnp.concatenate(
            [flag(spot == row_ref[ref : ref + 1, :]) for ref in range(REF)], axis=1
        )
        outgoing_ref[pl.ds(start, size), :] = fold(matmul(pick, given))
        return carry

    lax.fori_loop(0, slots // size, place, 0, unroll=4)


def finish_kernel(
    returned_ref, incoming_ref, ocean_ref, mixed_ref, kept_ref, out_ref, flux_ref, held_ref, sems
):
    del kept_ref
    devices = incoming_ref.shape[0]
    elements = flux_ref.shape[1] // GLL
    incoming = jnp.transpose(incoming_ref[...].astype(F32)).astype(I32)
    element = iota((elements, devices), 0)
    part = jnp.zeros((elements, 256), F32)
    for slot in range(0, CAP, 2):
        select = jnp.concatenate(
            [flag(element == incoming[slot + extra : slot + extra + 1, :]) for extra in range(2)],
            axis=1,
        )
        values = jnp.concatenate(
            [pair(returned_ref[pl.ds(slot + extra, devices, stride=CAP), :]) for extra in range(2)],
            axis=0,
        )
        part = part + matmul(select, values)
    swapped = turned_swap(fold(part))
    parts = sems.shape[0]
    size = held_ref.shape[0] // parts
    row, lane = iota((16, 256), 0) & 7, iota((16, 256), 1)
    first, second = (row == 0) & (lane == 0), (row == 6) & (lane == 128)
    picks = flag(first | second)
    tens, copies = [], []
    for index in range(parts):
        for start in range(index * size, index * size + size, 128):
            columns = slice(start, start + 128)
            flux = swapped[start // 16 : start // 16 + 8] + ocean_ref[:, columns]
            flux_ref[:, columns] = flux
            tens.append(0.1 * flux)
        high, low = high_low(jnp.concatenate(tens[-size // 128 :], axis=1))
        table = jnp.concatenate([high, low], axis=0).astype(BF16)
        added = lax.dot_general(
            table, picks, (((0,), (0,)), ((), ())), preferred_element_type=F32
        )
        rows = slice(index * size, index * size + size)
        held_ref[rows, :] = (mixed_ref[rows, :].astype(F32) + added).astype(BF16)
        span = pl.ds(index * size, size)
        copy = pltpu.make_async_copy(
            held_ref.at[span, :], out_ref.at[span, pl.ds(0, 256)], sems.at[index]
        )
        copy.start()
        copies.append(copy)
    for copy in copies:
        copy.wait()


def whole(*shape):
    return pl.BlockSpec(shape, lambda *_: (0,) * len(shape))


def params(mebibytes, axes=0):
    return pltpu.CompilerParams(
        vmem_limit_bytes=mebibytes * MIB,
        dimension_semantics=("arbitrary",) * axes if axes else None,
    )


def cost(flops, moved, hard=0):
    return pl.CostEstimate(flops=int(flops), bytes_accessed=int(moved), transcendentals=int(hard))


def mix(mixing, atm_state, half, out_half):
    columns = atm_state.shape[0]
    parts = 4
    apart = out_half is None
    return pl.pallas_call(
        functools.partial(mix_kernel, half, out_half),
        grid=(1,),
        in_specs=[
            pl.BlockSpec((2, LEV, LEV), lambda i: (half, 0, 0)),
            pl.BlockSpec(memory_space=pltpu.HBM),
        ],
        out_specs=whole(columns, 256) if apart else pl.BlockSpec(memory_space=pltpu.HBM),
        out_shape=jax.ShapeDtypeStruct((columns, 256 if apart else NV * LEV), BF16),
        scratch_shapes=[
            pltpu.VMEM((columns, 256), BF16),
            pltpu.SemaphoreType.DMA((parts,)),
            pltpu.SemaphoreType.DMA((parts,)),
        ],
        compiler_params=params(16, 1),
        cost_estimate=cost(columns * 256 * 256 * 2 * SUB, columns * 256 * 4, columns * 256 * SUB),
    )(mixing, atm_state)


def on_device(
    atm_state,
    profile,
    mixing,
    radiation,
    ocean_mask,
    tile_src,
    tile_elem,
    remap_w,
    slope_class,
    aspect_class,
    sky_view,
    albedo,
    sun_cos,
    sun_azimuth,
):
    devices = lax.axis_size("sect") * lax.axis_size("lane")
    columns = atm_state.shape[0]
    elements = columns // GLL
    tiles = tile_src.shape[0]
    slots = devices * CAP
    requests = tiles * REF

    wanted, slot_row, slot_col = pl.pallas_call(
        route_kernel,
        out_shape=(
            jax.ShapeDtypeStruct((devices, 128), I32),
            jax.ShapeDtypeStruct((REF, tiles), I32),
            jax.ShapeDtypeStruct((tiles, 2 * REF), I32),
        ),
        compiler_params=params(60),
    )(tile_src.T, tile_elem.T)
    wanted, atm_state = lax.optimization_barrier((wanted, atm_state))
    incoming = lax.all_to_all(wanted, AXES, split_axis=0, concat_axis=0, tiled=True)

    parts = 4
    forcing, blocks = pl.pallas_call(
        forcing_kernel,
        grid=(1,),
        in_specs=[
            whole(1, LEV),
            pl.BlockSpec(memory_space=pltpu.HBM),
            whole(4, columns),
        ],
        out_specs=(whole(NF, columns), whole(elements, 256)),
        out_shape=(
            jax.ShapeDtypeStruct((NF, columns), F32),
            jax.ShapeDtypeStruct((elements, 256), BF16),
        ),
        scratch_shapes=[
            pltpu.VMEM((columns, NV * LEV), BF16),
            pltpu.SemaphoreType.DMA((parts,)),
        ],
        compiler_params=params(58, 1),
        cost_estimate=cost(columns * 512 * 32 * 2, columns * 1024),
    )(profile.reshape(1, LEV), atm_state, radiation)
    incoming, forcing, blocks = lax.optimization_barrier((incoming, forcing, blocks))

    reply = pl.pallas_call(
        reply_kernel,
        grid=(1,),
        in_specs=[whole(devices, 128), whole(elements, 256)],
        out_specs=pl.BlockSpec(memory_space=pltpu.HBM),
        out_shape=jax.ShapeDtypeStruct((slots, 128), F32),
        scratch_shapes=[pltpu.VMEM((slots, 128), F32), pltpu.SemaphoreType.DMA((4,))],
        compiler_params=params(60, 1),
        cost_estimate=cost(slots * 256 * 256 * 2, slots * 512),
    )(incoming, blocks)
    reply, remap_w, slope_class, sun_cos = lax.optimization_barrier(
        (reply, remap_w, slope_class, sun_cos)
    )
    arrived = lax.all_to_all(
        reply.reshape(devices, CAP, 128), AXES, split_axis=0, concat_axis=0, tiled=True
    ).reshape(slots, 128)

    cosine = sun_cos[:, None]
    sine = jnp.sqrt(1.0 - cosine * cosine)
    slope_angle = slope_class.astype(F32) * 0.1
    aspect_angle = aspect_class.astype(F32) * (2.0 * math.pi / NASPECT)
    incidence = (
        jnp.maximum(
            0.0,
            jnp.cos(slope_angle) * cosine
            + jnp.sin(slope_angle) * sine * jnp.cos(sun_azimuth[:, None] - aspect_angle),
        )
        / cosine
    )
    rows = 4096
    both, inverse = pl.pallas_call(
        prepare_kernel,
        grid=(tiles * KDIM // rows,),
        in_specs=[pl.BlockSpec((rows, UNIT), lambda i: (i, 0))],
        out_specs=(
            pl.BlockSpec((rows, 256), lambda i: (i, 0)),
            pl.BlockSpec((rows // KDIM, UNIT), lambda i: (i, 0)),
        ),
        out_shape=(
            jax.ShapeDtypeStruct((tiles * KDIM, 256), BF16),
            jax.ShapeDtypeStruct((tiles, UNIT), F32),
        ),
        compiler_params=params(20, 1),
        cost_estimate=cost(tiles * KDIM * UNIT * 8, tiles * KDIM * UNIT * 8),
    )(remap_w.reshape(tiles * KDIM, UNIT))
    arrived, both, inverse, incidence = lax.optimization_barrier(
        (arrived, both, inverse, incidence)
    )

    land_temp, outgoing = pl.pallas_call(
        land_kernel,
        grid=(1,),
        in_specs=[
            whole(slots, 128),
            whole(REF, tiles),
            whole(tiles, 2 * REF),
            pl.BlockSpec(memory_space=pltpu.HBM),
            whole(tiles, UNIT),
            whole(tiles, UNIT),
            whole(tiles, UNIT),
            whole(tiles, UNIT),
        ],
        out_specs=(whole(tiles, UNIT), whole(slots, 128)),
        out_shape=(
            jax.ShapeDtypeStruct((tiles, UNIT), F32),
            jax.ShapeDtypeStruct((slots, 128), F32),
        ),
        scratch_shapes=[
            pltpu.VMEM((requests, 128), F32),
            pltpu.VMEM((tiles * NF, 128), F32),
            pltpu.VMEM((tiles * KDIM, 256), BF16),
            pltpu.SemaphoreType.DMA((4,)),
        ],
        compiler_params=params(50, 1),
        cost_estimate=cost(4 * requests * slots * 256 * 2, tiles * KDIM * UNIT * 4),
    )(arrived, slot_row, slot_col, both, inverse, incidence, sky_view, albedo)
    outgoing, atm_state, forcing = lax.optimization_barrier((outgoing, atm_state, forcing))
    returned = lax.all_to_all(
        outgoing.reshape(devices, CAP, 128), AXES, split_axis=0, concat_axis=0, tiled=True
    ).reshape(slots, 128)

    mixed = mix(mixing, atm_state, 0, None)
    kept = mix(mixing, atm_state, 1, 1)
    ocean = pl.pallas_call(
        ocean_kernel,
        out_shape=jax.ShapeDtypeStruct((NF, columns), F32),
        compiler_params=params(16),
        cost_estimate=cost(columns * 100, columns * 64, columns * 4),
    )(forcing, ocean_mask.reshape(1, columns))
    returned, mixed, kept, ocean = lax.optimization_barrier((returned, mixed, kept, ocean))

    atm_out, col_flux = pl.pallas_call(
        finish_kernel,
        grid=(1,),
        in_specs=[
            whole(slots, 128),
            whole(devices, 128),
            whole(NF, columns),
            whole(columns, 256),
            pl.BlockSpec(memory_space=pltpu.HBM),
        ],
        out_specs=(pl.BlockSpec(memory_space=pltpu.HBM), whole(NF, columns)),
        out_shape=(
            jax.ShapeDtypeStruct((columns, NV * LEV), BF16),
            jax.ShapeDtypeStruct((NF, columns), F32),
        ),
        scratch_shapes=[
            pltpu.VMEM((columns, 256), BF16),
            pltpu.SemaphoreType.DMA((8,)),
        ],
        input_output_aliases={4: 0},
        compiler_params=params(16, 1),
    )(returned, incoming, ocean, mixed, kept)
    return (atm_out, land_temp, col_flux)


def solution(mesh):
    return jax.shard_map(
        on_device,
        mesh=mesh,
        in_specs=(
            P(AXES, None),
            P(),
            P(),
            P(None, AXES),
            P(AXES),
            P(AXES, None),
            P(AXES, None),
            P(AXES, None, None),
            P(AXES, None),
            P(AXES, None),
            P(AXES, None),
            P(AXES, None),
            P(AXES),
            P(AXES),
        ),
        out_specs=(P(AXES, None), P(AXES, None), P(None, AXES)),
        check_vma=False,
    )
```
